512 devices in a mesh: dp: 32 (over y_lo, z), tensor: 16 (over y_hi, x, core).
Axes of the slice: x: 4, y: 4 (y_hi: 2, y_lo: 2; y = y_hi * 2 + y_lo), z: 16, core: 2. Of those that a mesh axis runs over, the one named last changes fastest.
Arguments:
- tokens: bfloat16 [8192, 6144], P(('dp', 'tensor')), may hold values from -6 to 6
- layer_norm_gain: float32 [6144], replicated, may hold values from 0.5 to 1.5
- input_weight: bfloat16 [6144, 12288], P('dp', 'tensor'), may hold values from -0.078125 to 0.078125
- adapter_down_weight: bfloat16 [8, 6144], replicated, may hold values from -0.078125 to 0.078125
- adapter_up_weight: bfloat16 [8, 12288], P(None, 'tensor'), may hold values from -1 to 1
- output_gradient: bfloat16 [8192, 6144], P(('dp', 'tensor')), may hold values from -6 to 6
- attention_gradient: bfloat16 [8192, 4096], P('dp', 'tensor'), may hold values from -6 to 6
Outputs:
- token_gradient: bfloat16 [8192, 6144], P(('dp', 'tensor'))
- grad_a: float32 [8, 6144], replicated
- grad_b: float32 [8, 12288], P(None, 'tensor')
The draws below stay inside these ranges and needn't reach their ends.
All inputs are finite; a program needn't handle non-finite values.
Results may differ from the reference program's by a relative error of at most 0.018.
Values may be sent and summed in bfloat16 or wider, within the bound.
A program may use at most 64 MiB of HBM per device.

```python
import math
import jax
import jax.numpy as jnp
from jax import lax

MODEL_WIDTH = 6144
HEAD = 128
HEADS_DEV = 2
ADAPTER_RANK = 8
SEQ = 256
TOKENS = 8192
JOINED_COLUMNS = 768
N_TENSOR = 16


def level_of(own_key, shape, cuts, low, high):
    def one(position, blocks):
        draws = jax.random.uniform(jax.random.fold_in(jax.random.fold_in(own_key, 6), position), (blocks,), jnp.float32, low / len(cuts), high / len(cuts))
        return jnp.repeat(jnp.exp(draws), shape[position] // blocks).reshape((-1,) + (1,) * (len(shape) - position - 1))

    factor_of = one(*cuts[0])
    for cut in cuts[1:]:
        factor_of = factor_of * one(*cut)
    return factor_of


def bell_draw(rng, dims, spread, reach, pieces=(), kind=jnp.bfloat16):
    entries = jax.random.normal(rng, dims, jnp.float32) * spread
    if len(pieces) > 0:
        entries = level_of(rng, dims, pieces, -0.22, 0.18) * entries
    return jnp.clip(entries, min=-reach, max=reach).astype(kind)


def setup_inputs(seed: int = 0) -> dict:
    arg_keys = jax.random.split(jax.random.key(seed), 8)
    tokens = bell_draw(arg_keys[0], (TOKENS, MODEL_WIDTH), 1.0, 6.0, ((0, 512),))
    layer_norm_gain = jnp.clip(1.0 + 0.1 * jax.random.normal(arg_keys[1], (MODEL_WIDTH,), jnp.float32), 0.5, 1.5)
    input_weight = bell_draw(arg_keys[2], (MODEL_WIDTH, N_TENSOR * JOINED_COLUMNS), MODEL_WIDTH ** -0.5, 0.078125, ((0, 32), (1, 16)))
    adapter_down_weight = bell_draw(arg_keys[3], (ADAPTER_RANK, MODEL_WIDTH), MODEL_WIDTH ** -0.5, 0.078125)
    adapter_up_weight = bell_draw(arg_keys[4], (ADAPTER_RANK, N_TENSOR * JOINED_COLUMNS), (4 * ADAPTER_RANK) ** -0.5, 1.0, ((1, 16),))
    output_gradient = bell_draw(arg_keys[5], (TOKENS, MODEL_WIDTH), 1.0, 6.0, ((0, 512),))
    attention_gradient = bell_draw(arg_keys[6], (TOKENS, N_TENSOR * HEADS_DEV * HEAD), 1.0, 6.0, ((0, 32), (1, 16)))
    return {"tokens": tokens, "layer_norm_gain": layer_norm_gain, "input_weight": input_weight, "adapter_down_weight": adapter_down_weight, "adapter_up_weight": adapter_up_weight, "output_gradient": output_gradient, "attention_gradient": attention_gradient}


EPSILON = 1e-06

def product_float32(first_op, second_op):
    return jnp.dot(first_op.astype(jnp.float32), second_op.astype(jnp.float32), preferred_element_type=jnp.float32)

def row_norm_value(values):
    row_mean = lax.optimization_barrier(jnp.mean(values, axis=-1, keepdims=True))
    centred = values - row_mean
    inverse_norm = lax.rsqrt(lax.optimization_barrier(jnp.mean(centred * centred, axis=-1, keepdims=True)) + EPSILON)
    return (centred * inverse_norm, inverse_norm)

def layer_norm_backward(gradient, normal, inverse_norm):
    return (gradient - lax.optimization_barrier(jnp.mean(gradient, axis=-1, keepdims=True)) - normal * lax.optimization_barrier(jnp.mean(gradient * normal, axis=-1, keepdims=True))) * inverse_norm

def reference(tokens, layer_norm_gain, input_weight, adapter_down_weight, adapter_up_weight, output_gradient, attention_gradient):
    row_total_sum = tokens.shape[0]
    column_groups = N_TENSOR
    head_span = HEADS_DEV * HEAD
    group_columns = 3 * head_span
    centred_normed_input, inverse_norm = row_norm_value(tokens.astype(jnp.float32))
    normed_input = (centred_normed_input * layer_norm_gain).astype(jnp.bfloat16)
    low_rank_input = product_float32(normed_input, adapter_down_weight.T).astype(jnp.bfloat16)
    joined_output = (product_float32(normed_input, input_weight) + product_float32(low_rank_input, adapter_up_weight)).reshape(row_total_sum, column_groups, group_columns)
    images = row_total_sum // SEQ
    head_shape = (images, SEQ, column_groups * HEADS_DEV, HEAD)
    query = joined_output[:, :, :head_span].reshape(head_shape)
    key_rows = joined_output[:, :, head_span:2 * head_span].reshape(head_shape)
    value_round = joined_output[:, :, 2 * head_span:].reshape(head_shape).astype(jnp.bfloat16)
    query_norm, query_scale = row_norm_value(query)
    key_norm, key_scale = row_norm_value(key_rows)
    query_round = query_norm.astype(jnp.bfloat16)
    key_round = key_norm.astype(jnp.bfloat16)
    score_scale = HEAD ** (-0.5)
    scores = jnp.einsum('bqhd,bkhd->bhqk', query_round.astype(jnp.float32), key_round.astype(jnp.float32)) * score_scale
    weights = jnp.exp(scores)
    attn_probs = weights / lax.optimization_barrier(jnp.sum(weights, axis=-1, keepdims=True))
    probs_round = attn_probs.astype(jnp.bfloat16)
    grad_att = attention_gradient.reshape(head_shape).astype(jnp.float32)
    grad_values = jnp.einsum('bhqk,bqhd->bkhd', probs_round.astype(jnp.float32), grad_att)
    grad_probs = jnp.einsum('bqhd,bkhd->bhqk', grad_att, value_round.astype(jnp.float32))
    grad_scores = attn_probs * (grad_probs - lax.optimization_barrier(jnp.sum(attn_probs * grad_probs, axis=-1, keepdims=True)))
    scores_round = (grad_scores * score_scale).astype(jnp.bfloat16).astype(jnp.float32)
    grad_qn = jnp.einsum('bhqk,bkhd->bqhd', scores_round, key_round.astype(jnp.float32))
    grad_kn = jnp.einsum('bhqk,bqhd->bkhd', scores_round, query_round.astype(jnp.float32))
    grad_query = layer_norm_backward(grad_qn, query_norm, query_scale)
    grad_key = layer_norm_backward(grad_kn, key_norm, key_scale)
    part_shape = (row_total_sum, column_groups, head_span)
    joined_gradient = jnp.concatenate([grad_query.reshape(part_shape), grad_key.reshape(part_shape), grad_values.reshape(part_shape)], axis=2)
    joined_gradient = joined_gradient.astype(jnp.bfloat16).reshape(row_total_sum, column_groups * group_columns)
    low_rank_gradient = product_float32(joined_gradient, adapter_up_weight.T).astype(jnp.bfloat16)

    def add_group(group_index, total):
        col_start = (group_index * group_columns).astype(jnp.int32)
        grad_part = lax.dynamic_slice_in_dim(joined_gradient, col_start, group_columns, 1)
        weight_part = lax.dynamic_slice_in_dim(input_weight, col_start, group_columns, 1)
        partial_sum = product_float32(grad_part, weight_part.T).astype(jnp.bfloat16)
        return total + lax.optimization_barrier(partial_sum).astype(jnp.float32)
    normed_gradient = lax.fori_loop(0, column_groups, add_group, jnp.zeros((row_total_sum, tokens.shape[1]), jnp.float32))
    normed_gradient = normed_gradient + product_float32(low_rank_gradient, adapter_down_weight)
    token_gradient = (output_gradient.astype(jnp.float32) + layer_norm_backward(normed_gradient * layer_norm_gain, centred_normed_input, inverse_norm)).astype(jnp.bfloat16)
    factor = 1.0 / math.sqrt(row_total_sum)
    grad_a = product_float32(low_rank_gradient.T, normed_input) * factor
    grad_b = product_float32(low_rank_input.T, joined_gradient) * factor
    return (token_gradient, grad_a, grad_b)
```

```python
import jax
import jax.numpy as jnp
from jax import lax
from jax.experimental import pallas as pl
from jax.experimental.pallas import tpu as pltpu
from jax.sharding import PartitionSpec as P

HEAD = 128
SEQ = 256
WIDTH = 6144
HALF = WIDTH // 2
RANK = 8
NZ = 16
ROWS = 192
COLS = 3 * HEAD
PARTS = 4
PART = HALF // PARTS
HP = PART // 2
PLANE = 512
EPSILON = 1e-06
F32 = jnp.float32
BF16 = jnp.bfloat16


def row_norm(values):
    mean = jnp.mean(values, axis=-1, keepdims=True)
    centred = values - mean
    inverse = lax.rsqrt(jnp.mean(centred * centred, axis=-1, keepdims=True) + EPSILON)
    return centred * inverse, inverse


def norm_backward(gradient, normal, inverse):
    return (
        gradient
        - jnp.mean(gradient, axis=-1, keepdims=True)
        - normal * jnp.mean(gradient * normal, axis=-1, keepdims=True)
    ) * inverse


def dot(a, b, ca=1, cb=0):
    return lax.dot_general(a, b, (((ca,), (cb,)), ((), ())), preferred_element_type=F32)


class Allocator:
    def __init__(self):
        self.size = 0

    def take(self, count):
        base = self.size
        self.size += count
        return base


def plan():
    al = Allocator()
    names = dict(
        wy=1, do=1, ring=32, t1=6, t2=6, t3=2,
        sib=2 * PARTS, r1=4 * PARTS, r2=4 * PARTS, r3=4 * PARTS, r4=4 * PARTS,
        g0=1, g1=3, g2=3, z1=3, z2=3, ax=3, ay=3, by=1,
    )
    bases = {name: al.take(count) for name, count in names.items()}
    return bases, al.size


SEM, N_SEM = plan()


def kernel(
    tok, gain, w, down, up, og, dout,
    o_tok, o_a, o_b,
    norm, wf, wst, acc, dall, xhat, inv, dpad, upad, lowr,
    gj, gl, sib_s, sib_r, own, part, r1, r2, tot, r3, r4, gn,
    gls, glx, gly, z1, z2, ga, gb,
    ssem, rsem,
):
    dp = lax.axis_index("dp")
    tt = lax.axis_index("tensor")
    yl, z = lax.div(dp, NZ), lax.rem(dp, NZ)
    yh = lax.div(tt, 8)
    x = lax.rem(lax.div(tt, 2), 4)
    c = lax.rem(tt, 2)
    y = 2 * yh + yl
    zh, zl = lax.div(z, 4), lax.rem(z, 4)
    other_c = 1 - c
    other_y = 1 - yl

    def at(y_, x_, z_, c_):
        return (
            lax.rem(y_, 2) * NZ + z_,
            lax.div(y_, 2) * 8 + x_ * 2 + c_,
        )

    xs = [at(y, lax.rem(x + d, 4), z, c) for d in (1, 2, 3)]
    ys = [at(lax.rem(y + d, 4), x, z, c) for d in (1, 2, 3)]
    zu = at(y, x, lax.rem(z + 1, NZ), c)
    zd = at(y, x, lax.rem(z + NZ - 1, NZ), c)
    zq = [at(y, x, zh * 4 + lax.rem(zl + d, 4), c) for d in (1, 2, 3)]
    zs = [at(y, x, lax.rem(zh + d, 4) * 4 + zl, c) for d in (1, 2, 3)]
    mate = at(y, x, z, other_c)
    pair = at(2 * yh + other_y, x, z, c)
    peers = [mate, *xs, *ys, zu, zd, *zq, *zs]

    def copy(src, dst, k, device):
        return pltpu.make_async_remote_copy(
            src_ref=src, dst_ref=dst, send_sem=ssem.at[k], recv_sem=rsem.at[k],
            device_id=device, device_id_type=pl.DeviceIdType.MESH,
        )

    pending = []

    def send(src, dst, k, device):
        one = copy(src, dst, k, device)
        one.start()
        pending.append(one)

    def arrived(ref, k):
        copy(ref, ref, k, mate).wait_recv()

    def flush(keep=0):
        while len(pending) > keep:
            pending.pop(0).wait_send()

    barrier = pltpu.get_barrier_semaphore()
    for device in peers:
        pl.semaphore_signal(barrier, inc=1, device_id=device, device_id_type=pl.DeviceIdType.MESH)

    for h in range(2):
        for j in range(3):
            wst[h, :, 128 * j : 128 * j + 128] = w[:, 256 * j + 128 * h : 256 * j + 128 * h + 128]
    wf[yl, z] = wst[yl]
    normal, inverse = row_norm(tok[...].astype(F32))
    xhat[...] = normal
    inv[...] = jnp.broadcast_to(inverse, inv.shape)
    norm[yl, yh, x, c] = (normal * gain[...]).astype(BF16)

    pl.semaphore_wait(barrier, len(peers))

    own_cols = pl.ds(pl.multiple_of(yl * HEAD, HEAD), HEAD)
    pair_cols = pl.ds(pl.multiple_of(other_y * HEAD, HEAD), HEAD)
    send(wst.at[other_y], wf.at[yl, z], SEM["wy"], pair)

    def ring_index(way, step, j):
        return SEM["ring"] + way * 16 + (step - 1) * 2 + j

    def ring_send(way, step, j):
        block = lax.rem(z + NZ - (step - 1), NZ) if way == 0 else lax.rem(z + step - 1, NZ)
        ref = wf.at[j, block]
        send(ref, ref, ring_index(way, step, j), zu if way == 0 else zd)

    def ring_wait(way, step, j):
        block = lax.rem(z + NZ - step, NZ) if way == 0 else lax.rem(z + step, NZ)
        arrived(wf.at[j, block], ring_index(way, step, j))

    for way in range(2):
        ring_send(way, 1, yl)
    a_cols, b_cols = pl.ds(0, HALF), pl.ds(HALF, HALF)
    a_ref = norm.at[yl, yh, x, c, :, a_cols]
    b_ref = norm.at[yl, yh, x, c, :, b_cols]
    for d in range(3):
        send(a_ref, a_ref, SEM["t1"] + d, xs[d])
        send(b_ref, b_ref, SEM["t1"] + 3 + d, ys[d])
    send(dout.at[:, pair_cols], dall.at[yl], SEM["do"], pair)
    dall[yl] = dout[:, own_cols]

    dpad[...] = jnp.concatenate([down[...].astype(F32), jnp.zeros((8, WIDTH), F32)], axis=0).astype(BF16)
    for j in range(3):
        cols = pl.ds(pl.multiple_of(256 * j + yl * HEAD, HEAD), HEAD)
        upad[:, 128 * j : 128 * j + 128] = jnp.concatenate(
            [up[:, cols].astype(F32), jnp.zeros((8, HEAD), F32)], axis=0
        ).astype(BF16)

    arrived(wf.at[other_y, z], SEM["wy"])
    for way in range(2):
        ring_send(way, 1, other_y)

    def forward(step):
        up_way = lax.rem(step + z, 2)
        base = lax.rem(up_way * (z + step - 1) + (1 - up_way) * (z - step + NZ), NZ)
        block = lax.div(base, 2)
        for j in range(2):
            lanes = pl.ds(pl.multiple_of(HALF * j + 2 * ROWS * block, 128), 2 * ROWS)
            left = norm[:, :, :, :, :, lanes].reshape(PLANE, 2 * ROWS)
            right = wf[j, pl.ds(2 * block, 2)].reshape(2 * ROWS, COLS)
            acc[...] += dot(left, right)

    def tokens_second():
        for d in range(3):
            xd, yd = lax.rem(x + 3 - d, 4), lax.rem(y + 3 - d, 4)
            arrived(norm.at[yl, yh, xd, c, :, a_cols], SEM["t1"] + d)
            arrived(norm.at[lax.rem(yd, 2), lax.div(yd, 2), x, c, :, b_cols], SEM["t1"] + 3 + d)
        ra = norm.at[yl, yh, :, c, :, a_cols]
        rb = norm.at[:, :, x, c, :, b_cols]
        for d in range(3):
            send(ra, ra, SEM["t2"] + d, ys[d])
            send(rb, rb, SEM["t2"] + 3 + d, xs[d])

    def tokens_mate():
        for d in range(3):
            yd = lax.rem(y + 3 - d, 4)
            arrived(norm.at[lax.rem(yd, 2), lax.div(yd, 2), :, c, :, a_cols], SEM["t2"] + d)
        ref = norm.at[:, :, :, c, :, a_cols]
        send(ref, ref, SEM["t3"], mate)
        for d in range(3):
            xd = lax.rem(x + 3 - d, 4)
            arrived(norm.at[:, :, xd, c, :, b_cols], SEM["t2"] + 3 + d)
        ref = norm.at[:, :, :, c, :, b_cols]
        send(ref, ref, SEM["t3"] + 1, mate)

    def tokens_done():
        arrived(norm.at[:, :, :, other_c, :, a_cols], SEM["t3"])
        arrived(norm.at[:, :, :, other_c, :, b_cols], SEM["t3"] + 1)

    for step in range(2, 9):
        if step < 8:
            for j in (yl, other_y):
                for way in range(2):
                    ring_wait(way, step - 1, j)
                    ring_send(way, step, j)
        else:
            ring_wait(0, 7, 0)
            ring_send(0, 8, 0)
            ring_wait(1, 7, 1)
            ring_send(1, 8, 1)
            ring_wait(0, 7, 1)
            ring_wait(1, 7, 0)
        if step == 2:
            tokens_second()
        if step == 5:
            tokens_mate()
        if step == 6:
            tokens_done()
            low = dot(norm[...].reshape(PLANE, WIDTH), dpad[...], 1, 1).astype(BF16)
            lowr[...] = low
            acc[...] = dot(low, upad[...])

            def several(s, carry):
                forward(s)
                return carry

            lax.fori_loop(1, 6, several, 0)
        if step == 7:
            forward(6)
        if step == 8:
            forward(7)
    arrived(dall.at[other_y], SEM["do"])
    flush(8)
    ring_wait(0, 8, 0)
    ring_wait(1, 8, 1)
    forward(8)

    scale = HEAD ** (-0.5)
    for i in range(2):
        rows = slice(SEQ * i, SEQ * i + SEQ)
        q_norm, q_inv = row_norm(acc[rows, 0:128])
        k_norm, k_inv = row_norm(acc[rows, 128:256])
        value = acc[rows, 256:384].astype(BF16)
        query, key = q_norm.astype(BF16), k_norm.astype(BF16)
        weights = jnp.exp(dot(query, key, 1, 1) * scale)
        probs = weights / jnp.sum(weights, axis=-1, keepdims=True)
        cot = dall[i]
        g_value = dot(probs.astype(BF16), cot, 0, 0)
        g_probs = dot(cot, value, 1, 1)
        g_scores = probs * (g_probs - jnp.sum(probs * g_probs, axis=-1, keepdims=True))
        g_scores = (g_scores * scale).astype(BF16)
        g_query = norm_backward(dot(g_scores, key), q_norm, q_inv)
        g_key = norm_backward(dot(g_scores, query, 0, 0), k_norm, k_inv)
        joined = jnp.concatenate([g_query, g_key, g_value], axis=1).astype(BF16)
        low = dot(joined, upad[...], 1, 1).astype(BF16)
        gls[c, :, SEQ * i : SEQ * i + SEQ] = dot(upad[...], joined, 1, 1)[0:RANK]
        if i == 0:
            b_part = dot(lowr[rows], joined, 0, 0)
        else:
            b_part = b_part + dot(lowr[rows], joined, 0, 0)
        for bh in range(2):
            for bx in range(4):
                for bc in range(2):
                    r = 16 * (8 * bh + 2 * bx + bc)
                    by = 2 * bh + i
                    rel = lax.rem(c + bc, 2)
                    gj[0, rel, bx, by] = joined[r : r + 16]
                    gj[1, rel, by, bx] = joined[r : r + 16]
                    gl[0, rel, bx, by] = low[r : r + 16]
                    gl[1, rel, by, bx] = low[r : r + 16]
    b_part = b_part[0:RANK]
    send(gls.at[c], gls.at[c], SEM["g0"], mate)

    place = [(x, y), (y, x)]
    near = [
        ((xs[0], xs[2]), (ys[0], ys[2])),
        ((ys[0], ys[2]), (xs[0], xs[2])),
    ]
    lo, hi = pl.ds(0, HP), pl.ds(HP, HP)

    def stage_product(i):
        for h in range(2):
            right = wf[h, 4 * i : 4 * i + 4].reshape(PART, COLS)
            low = dpad[:, HALF * h + PART * i : HALF * h + PART * i + PART]
            for rel in (1, 0):
                left = gj[h, rel].reshape(SEQ, COLS)
                out = dot(left, right, 1, 1) + dot(gl[h, rel].reshape(SEQ, 16), low)
                out = out.reshape(4, 4, 16, PART)
                if rel == 1:
                    sib_s[h, i] = out.astype(BF16)
                    send(sib_s.at[h, i], sib_r.at[h, i], SEM["sib"] + h * PARTS + i, mate)
                else:
                    own[h, i] = out

    def index(name, h, i, way):
        return SEM[name] + (h * PARTS + i) * 2 + way

    def stage_mate(i):
        for h in range(2):
            arrived(sib_r.at[h, i], SEM["sib"] + h * PARTS + i)
            part[h, i] = (own[h, i] + sib_r[h, i].astype(F32)).astype(BF16)
            far = lax.rem(place[h][0] + 2, 4)
            send(part.at[h, i, far, :, :, lo], r1.at[h, i, 0], index("r1", h, i, 0), near[h][0][0])
            send(part.at[h, i, far, :, :, hi], r1.at[h, i, 1], index("r1", h, i, 1), near[h][0][1])

    def stage_one(i):
        for h in range(2):
            me = place[h][0]
            nxt, prv = lax.rem(me + 1, 4), lax.rem(me + 3, 4)
            arrived(r1.at[h, i, 0], index("r1", h, i, 0))
            part[h, i, nxt, :, :, 0:HP] = (
                part[h, i, nxt, :, :, 0:HP].astype(F32) + r1[h, i, 0].astype(F32)
            ).astype(BF16)
            send(part.at[h, i, nxt], r2.at[h, i, 0], index("r2", h, i, 0), near[h][0][0])
            arrived(r1.at[h, i, 1], index("r1", h, i, 1))
            part[h, i, prv, :, :, HP:PART] = (
                part[h, i, prv, :, :, HP:PART].astype(F32) + r1[h, i, 1].astype(F32)
            ).astype(BF16)
            send(part.at[h, i, prv], r2.at[h, i, 1], index("r2", h, i, 1), near[h][0][1])

    def stage_two(i):
        for h in range(2):
            me, across = place[h]
            arrived(r2.at[h, i, 0], index("r2", h, i, 0))
            arrived(r2.at[h, i, 1], index("r2", h, i, 1))
            tot[h, i] = (
                part[h, i, me].astype(F32) + r2[h, i, 0].astype(F32) + r2[h, i, 1].astype(F32)
            ).astype(BF16)
            far = lax.rem(across + 2, 4)
            send(tot.at[h, i, far, :, lo], r3.at[h, i, 0], index("r3", h, i, 0), near[h][1][0])
            send(tot.at[h, i, far, :, hi], r3.at[h, i, 1], index("r3", h, i, 1), near[h][1][1])

    def stage_three(i):
        for h in range(2):
            me = place[h][1]
            nxt, prv = lax.rem(me + 1, 4), lax.rem(me + 3, 4)
            arrived(r3.at[h, i, 0], index("r3", h, i, 0))
            tot[h, i, nxt, :, 0:HP] = (
                tot[h, i, nxt, :, 0:HP].astype(F32) + r3[h, i, 0].astype(F32)
            ).astype(BF16)
            send(tot.at[h, i, nxt], r4.at[h, i, 0], index("r4", h, i, 0), near[h][1][0])
            arrived(r3.at[h, i, 1], index("r3", h, i, 1))
            tot[h, i, prv, :, HP:PART] = (
                tot[h, i, prv, :, HP:PART].astype(F32) + r3[h, i, 1].astype(F32)
            ).astype(BF16)
            send(tot.at[h, i, prv], r4.at[h, i, 1], index("r4", h, i, 1), near[h][1][1])

    def stage_four(i):
        for h in range(2):
            me = place[h][1]
            arrived(r4.at[h, i, 0], index("r4", h, i, 0))
            arrived(r4.at[h, i, 1], index("r4", h, i, 1))
            cols = slice(HALF * h + PART * i, HALF * h + PART * i + PART)
            gn[:, cols] = (
                tot[h, i, me].astype(F32) + r4[h, i, 0].astype(F32) + r4[h, i, 1].astype(F32)
            )

    factor = float(SEQ * 32) ** (-0.5)

    def spread(ref, slot, name, devices):
        for d in range(3):
            send(ref.at[slot], ref.at[slot], SEM[name] + d, devices[d])

    def gathered(ref, slot, name):
        for d in range(3):
            arrived(ref.at[lax.rem(slot + 3 - d, 4)], SEM[name] + d)

    def small(step):
        if step == 0:
            arrived(gls.at[other_c], SEM["g0"])
            glx[x] = gls[0] + gls[1]
            spread(glx, x, "g1", xs)
        if step == 1:
            gathered(glx, x, "g1")
            gly[y] = glx[0] + glx[1] + glx[2] + glx[3]
            spread(gly, y, "g2", ys)
        if step == 2:
            gathered(gly, y, "g2")
            low = gly[0] + gly[1] + gly[2] + gly[3]
            low = jnp.concatenate([low, jnp.zeros((8, PLANE), F32)], axis=0).astype(BF16)
            lanes = pl.ds(pl.multiple_of(384 * (4 * y + x), 128), 384)
            a_part = dot(low, norm[:, :, :, :, :, lanes].reshape(PLANE, 384))[0:RANK]
            z1[zl, 0:RANK] = a_part
            z1[zl, RANK : 2 * RANK] = b_part
            spread(z1, zl, "z1", zq)
        if step == 3:
            gathered(z1, zl, "z1")
            z2[zh] = z1[0] + z1[1] + z1[2] + z1[3]
            spread(z2, zh, "z2", zs)
        if step == 4:
            gathered(z2, zh, "z2")
            total = (z2[0] + z2[1] + z2[2] + z2[3]) * factor
            ga[y, x] = total[0:RANK]
            gb[yl] = total[RANK : 2 * RANK]
            send(gb.at[yl], gb.at[yl], SEM["by"], pair)
            for d in range(3):
                send(ga.at[y, x], ga.at[y, x], SEM["ax"] + d, xs[d])
        if step == 5:
            for d in range(3):
                arrived(ga.at[y, lax.rem(x + 3 - d, 4)], SEM["ax"] + d)
            spread(ga, y, "ay", ys)
        if step == 6:
            arrived(gb.at[other_y], SEM["by"])
            for h in range(2):
                for j in range(3):
                    o_b[:, 256 * j + 128 * h : 256 * j + 128 * h + 128] = gb[h, :, 128 * j : 128 * j + 128]
            gathered(ga, y, "ay")
            for a in range(4):
                for b in range(4):
                    k = 384 * (4 * a + b)
                    o_a[:, k : k + 384] = ga[a, b]

    stages = [stage_product, stage_mate, stage_one, stage_two, stage_three, stage_four]
    for t in range(PARTS + len(stages) - 1):
        for s in reversed(range(len(stages))):
            if 0 <= t - s < PARTS:
                stages[s](t - s)
        small(t)
        flush(24)

    gradient = gn[...] * gain[...]
    normal = xhat[...]
    out = norm_backward(gradient, normal, inv[:, 0:1])
    o_tok[...] = (og[...].astype(F32) + out).astype(BF16)
    flush()


def per_device(tokens, gain, weight, down, up, out_gradient, att_gradient):
    vmem = pl.BlockSpec(memory_space=pltpu.VMEM)
    shapes = [
        ((2, 2, 4, 2, 16, WIDTH), BF16),
        ((2, NZ, ROWS, COLS), BF16),
        ((2, ROWS, COLS), BF16),
        ((PLANE, COLS), F32),
        ((2, SEQ, HEAD), BF16),
        ((16, WIDTH), F32),
        ((16, HEAD), F32),
        ((16, WIDTH), BF16),
        ((16, COLS), BF16),
        ((PLANE, 16), BF16),
        ((2, 2, 4, 4, 16, COLS), BF16),
        ((2, 2, 4, 4, 16, 16), BF16),
        ((2, PARTS, 4, 4, 16, PART), BF16),
        ((2, PARTS, 4, 4, 16, PART), BF16),
        ((2, PARTS, 4, 4, 16, PART), F32),
        ((2, PARTS, 4, 4, 16, PART), BF16),
        ((2, PARTS, 2, 4, 16, HP), BF16),
        ((2, PARTS, 2, 4, 16, PART), BF16),
        ((2, PARTS, 4, 16, PART), BF16),
        ((2, PARTS, 2, 16, HP), BF16),
        ((2, PARTS, 2, 16, PART), BF16),
        ((16, WIDTH), F32),
        ((2, RANK, PLANE), F32),
        ((4, RANK, PLANE), F32),
        ((4, RANK, PLANE), F32),
        ((4, 2 * RANK, COLS), F32),
        ((4, 2 * RANK, COLS), F32),
        ((4, 4, RANK, 384), F32),
        ((2, RANK, COLS), F32),
    ]
    scratch = [pltpu.VMEM(shape, kind) for shape, kind in shapes]
    scratch += [pltpu.SemaphoreType.DMA((N_SEM,)), pltpu.SemaphoreType.DMA((N_SEM,))]
    return pl.pallas_call(
        kernel,
        out_shape=(
            jax.ShapeDtypeStruct((16, WIDTH), BF16),
            jax.ShapeDtypeStruct((RANK, WIDTH), F32),
            jax.ShapeDtypeStruct((RANK, 2 * COLS), F32),
        ),
        in_specs=[vmem] * 7,
        out_specs=(vmem, vmem, vmem),
        scratch_shapes=scratch,
        compiler_params=pltpu.CompilerParams(
            collective_id=0, has_side_effects=True, vmem_limit_bytes=52 * 1024 * 1024
        ),
    )(tokens, gain.reshape(1, WIDTH), weight, down, up, out_gradient, att_gradient)


def solution(mesh):
    placed = (
        P(("dp", "tensor"), None),
        P(),
        P("dp", "tensor"),
        P(),
        P(None, "tensor"),
        P(("dp", "tensor"), None),
        P("dp", "tensor"),
    )
    return jax.shard_map(
        per_device,
        mesh=mesh,
        in_specs=placed,
        out_specs=(P(("dp", "tensor"), None), P(), P(None, "tensor")),
        check_vma=False,
    )
```

```python
import jax
import jax.numpy as jnp
from jax import lax
from jax.experimental import pallas as pl
from jax.experimental.pallas import tpu as pltpu
from jax.sharding import PartitionSpec as P

HEAD = 128
SEQ = 256
WIDTH = 6144
HALF = WIDTH // 2
RANK = 8
NZ = 16
ROWS = 192
COLS = 3 * HEAD
PARTS = 4
PART = HALF // PARTS
HP = PART // 2
PLANE = 512
EPSILON = 1e-06
F32 = jnp.float32
BF16 = jnp.bfloat16


def row_norm(values):
    mean = jnp.mean(values, axis=-1, keepdims=True)
    centred = values - mean
    inverse = lax.rsqrt(jnp.mean(centred * centred, axis=-1, keepdims=True) + EPSILON)
    return centred * inverse, inverse


def norm_backward(gradient, normal, inverse):
    return (
        gradient
        - jnp.mean(gradient, axis=-1, keepdims=True)
        - normal * jnp.mean(gradient * normal, axis=-1, keepdims=True)
    ) * inverse


def dot(a, b, ca=1, cb=0):
    return lax.dot_general(a, b, (((ca,), (cb,)), ((), ())), preferred_element_type=F32)


class Allocator:
    def __init__(self):
        self.size = 0

    def take(self, count):
        base = self.size
        self.size += count
        return base


def plan():
    al = Allocator()
    names = dict(
        wy=3, do=1, ring=32, t1=6, t2=6, t3=2,
        sib=6 * PARTS, r1=4 * PARTS, r2=4 * PARTS, r3=6 * PARTS,
        g0=1, g1=3, g2=3, z1=3, z2=3, ax=15, by=1,
    )
    bases = {name: al.take(count) for name, count in names.items()}
    return bases, al.size


SEM, N_SEM = plan()


def kernel(
    tok_in, gain_in, w_in, down_in, up_in, og_in, dout_in,
    o_tok, o_a, o_b,
    tok, gain, down, up, og,
    norm, wf, acc, dall, xhat, inv, dpad, upad, lowr,
    gj, sib_s, sib_r, own, far, r1, beside, r2, tot, r3, gn,
    gls, glx, gly, z1, z2, ga, gb,
    ssem, rsem, lsem,
):
    dp = lax.axis_index("dp")
    tt = lax.axis_index("tensor")
    yl, z = lax.div(dp, NZ), lax.rem(dp, NZ)
    yh = lax.div(tt, 8)
    x = lax.rem(lax.div(tt, 2), 4)
    c = lax.rem(tt, 2)
    y = 2 * yh + yl
    zh, zl = lax.div(z, 4), lax.rem(z, 4)
    other_c = 1 - c
    other_y = 1 - yl

    def at(y_, x_, z_, c_):
        return (
            lax.rem(y_, 2) * NZ + z_,
            lax.div(y_, 2) * 8 + x_ * 2 + c_,
        )

    xs = [at(y, lax.rem(x + d, 4), z, c) for d in (1, 2, 3)]
    ys = [at(lax.rem(y + d, 4), x, z, c) for d in (1, 2, 3)]
    zu = at(y, x, lax.rem(z + 1, NZ), c)
    zd = at(y, x, lax.rem(z + NZ - 1, NZ), c)
    zq = [at(y, x, zh * 4 + lax.rem(zl + d, 4), c) for d in (1, 2, 3)]
    zs = [at(y, x, lax.rem(zh + d, 4) * 4 + zl, c) for d in (1, 2, 3)]
    mate = at(y, x, z, other_c)
    pair = at(2 * yh + other_y, x, z, c)
    plane = [(a, b) for a in range(4) for b in range(4) if a + b > 0]
    across = [at(lax.rem(y + a, 4), lax.rem(x + b, 4), z, c) for a, b in plane]
    peers = [mate, *across, zu, zd, *zq, *zs]

    def copy(src, dst, k, device):
        return pltpu.make_async_remote_copy(
            src_ref=src, dst_ref=dst, send_sem=ssem.at[k], recv_sem=rsem.at[k],
            device_id=device, device_id_type=pl.DeviceIdType.MESH,
        )

    pending = []

    def send(src, dst, k, device):
        one = copy(src, dst, k, device)
        one.start()
        pending.append(one)

    def arrived(ref, k):
        copy(ref, ref, k, mate).wait_recv()

    def flush(keep=0):
        while len(pending) > keep:
            pending.pop(0).wait_send()

    barrier = pltpu.get_barrier_semaphore()
    for device in peers:
        pl.semaphore_signal(barrier, inc=1, device_id=device, device_id_type=pl.DeviceIdType.MESH)

    own_cols = pl.ds(pl.multiple_of(yl * HEAD, HEAD), HEAD)
    pair_cols = pl.ds(pl.multiple_of(other_y * HEAD, HEAD), HEAD)
    locals_ = []

    def fetch(src, dst):
        one = pltpu.make_async_copy(src, dst, lsem.at[len(locals_)])
        one.start()
        locals_.append(one)
        return one

    get_w = []
    for j in range(3):
        cols = pl.ds(pl.multiple_of(256 * j + yl * HEAD, HEAD), HEAD)
        get_w.append(fetch(w_in.at[:, cols], wf.at[yl, z, :, pl.ds(128 * j, 128)]))
    get_tok = [fetch(tok_in, tok), fetch(gain_in, gain)]
    get_small = [fetch(down_in, down), fetch(up_in, up), fetch(dout_in.at[:, own_cols], dall.at[yl])]
    get_og = fetch(og_in, og)

    pl.semaphore_wait(barrier, len(peers))

    for j in range(3):
        cols = pl.ds(pl.multiple_of(256 * j + other_y * HEAD, HEAD), HEAD)
        send(w_in.at[:, cols], wf.at[yl, z, :, pl.ds(128 * j, 128)], SEM["wy"] + j, pair)
    for one in get_w:
        one.wait()

    def ring_index(way, step, j):
        return SEM["ring"] + way * 16 + (step - 1) * 2 + j

    def ring_send(way, step, j):
        block = lax.rem(z + NZ - (step - 1), NZ) if way == 0 else lax.rem(z + step - 1, NZ)
        ref = wf.at[j, block]
        send(ref, ref, ring_index(way, step, j), zu if way == 0 else zd)

    def ring_wait(way, step, j):
        block = lax.rem(z + NZ - step, NZ) if way == 0 else lax.rem(z + step, NZ)
        arrived(wf.at[j, block], ring_index(way, step, j))

    for way in range(2):
        ring_send(way, 1, yl)
    for one in get_tok:
        one.wait()
    normal, inverse = row_norm(tok[...].astype(F32))
    xhat[...] = normal
    inv[...] = jnp.broadcast_to(inverse, inv.shape)
    norm[yl, yh, x, c] = (normal * gain[...]).astype(BF16)

    a_cols, b_cols = pl.ds(0, HALF), pl.ds(HALF, HALF)
    a_ref = norm.at[yl, yh, x, c, :, a_cols]
    b_ref = norm.at[yl, yh, x, c, :, b_cols]
    for d in range(3):
        send(a_ref, a_ref, SEM["t1"] + d, xs[d])
        send(b_ref, b_ref, SEM["t1"] + 3 + d, ys[d])
    send(dout_in.at[:, pair_cols], dall.at[yl], SEM["do"], pair)
    for one in get_small:
        one.wait()

    dpad[...] = jnp.concatenate([down[...].astype(F32), jnp.zeros((8, WIDTH), F32)], axis=0).astype(BF16)
    for j in range(3):
        cols = pl.ds(pl.multiple_of(256 * j + yl * HEAD, HEAD), HEAD)
        upad[:, 128 * j : 128 * j + 128] = jnp.concatenate(
            [up[:, cols].astype(F32), jnp.zeros((8, HEAD), F32)], axis=0
        ).astype(BF16)

    for j in range(3):
        arrived(wf.at[other_y, z, :, pl.ds(128 * j, 128)], SEM["wy"] + j)
    for way in range(2):
        ring_send(way, 1, other_y)

    def forward(step):
        up_way = lax.rem(step + z, 2)
        base = lax.rem(up_way * (z + step - 1) + (1 - up_way) * (z - step + NZ), NZ)
        block = lax.div(base, 2)
        for j in range(2):
            lanes = pl.ds(pl.multiple_of(HALF * j + 2 * ROWS * block, 128), 2 * ROWS)
            left = norm[:, :, :, :, :, lanes].reshape(PLANE, 2 * ROWS)
            right = wf[j, pl.ds(2 * block, 2)].reshape(2 * ROWS, COLS)
            acc[...] += dot(left, right)

    def tokens_second():
        for d in range(3):
            xd, yd = lax.rem(x + 3 - d, 4), lax.rem(y + 3 - d, 4)
            arrived(norm.at[yl, yh, xd, c, :, a_cols], SEM["t1"] + d)
            arrived(norm.at[lax.rem(yd, 2), lax.div(yd, 2), x, c, :, b_cols], SEM["t1"] + 3 + d)
        ra = norm.at[yl, yh, :, c, :, a_cols]
        rb = norm.at[:, :, x, c, :, b_cols]
        for d in range(3):
            send(ra, ra, SEM["t2"] + d, ys[d])
            send(rb, rb, SEM["t2"] + 3 + d, xs[d])

    def tokens_mate():
        for d in range(3):
            yd = lax.rem(y + 3 - d, 4)
            arrived(norm.at[lax.rem(yd, 2), lax.div(yd, 2), :, c, :, a_cols], SEM["t2"] + d)
        ref = norm.at[:, :, :, c, :, a_cols]
        send(ref, ref, SEM["t3"], mate)
        for d in range(3):
            xd = lax.rem(x + 3 - d, 4)
            arrived(norm.at[:, :, xd, c, :, b_cols], SEM["t2"] + 3 + d)
        ref = norm.at[:, :, :, c, :, b_cols]
        send(ref, ref, SEM["t3"] + 1, mate)

    def tokens_done():
        arrived(norm.at[:, :, :, other_c, :, a_cols], SEM["t3"])
        arrived(norm.at[:, :, :, other_c, :, b_cols], SEM["t3"] + 1)

    def forward_first():
        low = dot(norm[...].reshape(PLANE, WIDTH), dpad[...], 1, 1).astype(BF16)
        lowr[...] = low
        acc[...] = dot(low, upad[...])

        def several(s, carry):
            forward(s)
            return carry

        lax.fori_loop(1, 6, several, 0)

    def ring_step(step):
        if step < 8:
            for j in (yl, other_y):
                for way in range(2):
                    ring_wait(way, step - 1, j)
                    ring_send(way, step, j)
        elif step == 8:
            ring_wait(0, 7, 0)
            ring_send(0, 8, 0)
            ring_wait(1, 7, 1)
            ring_send(1, 8, 1)
            ring_wait(0, 7, 1)
            ring_wait(1, 7, 0)
        else:
            ring_wait(0, 8, 0)
            ring_wait(1, 8, 1)

    def dout_done():
        arrived(dall.at[other_y], SEM["do"])
        flush(8)

    for step in range(2, 10):
        ring_step(step)
        if step == 2:
            tokens_second()
        if step == 5:
            tokens_mate()
        if step == 6:
            tokens_done()
            forward_first()
        if step == 7:
            forward(6)
        if step == 8:
            forward(7)
            dout_done()
        if step == 9:
            forward(8)

    def order(to, me):
        d = lax.rem(to - me + 6, 4)
        return lax.rem(2 * d, 5) - lax.div(d, 2) * (1 - lax.div(d, 3))

    scale = HEAD ** (-0.5)
    def attention():
        for i in range(2):
            rows = slice(SEQ * i, SEQ * i + SEQ)
            q_norm, q_inv = row_norm(acc[rows, 0:128])
            k_norm, k_inv = row_norm(acc[rows, 128:256])
            value = acc[rows, 256:384].astype(BF16)
            query, key = q_norm.astype(BF16), k_norm.astype(BF16)
            weights = jnp.exp(dot(query, key, 1, 1) * scale)
            probs = weights / jnp.sum(weights, axis=-1, keepdims=True)
            cot = dall[i]
            g_value = dot(probs.astype(BF16), cot, 0, 0)
            g_probs = dot(cot, value, 1, 1)
            g_scores = probs * (g_probs - jnp.sum(probs * g_probs, axis=-1, keepdims=True))
            g_scores = (g_scores * scale).astype(BF16)
            g_query = norm_backward(dot(g_scores, key), q_norm, q_inv)
            g_key = norm_backward(dot(g_scores, query, 0, 0), k_norm, k_inv)
            joined = jnp.concatenate([g_query, g_key, g_value], axis=1).astype(BF16)
            gls[c, :, SEQ * i : SEQ * i + SEQ] = dot(upad[...], joined, 1, 1)[0:RANK]
            if i == 0:
                b_part = dot(lowr[rows], joined, 0, 0)
            else:
                b_part = b_part + dot(lowr[rows], joined, 0, 0)
            for bh in range(2):
                for bx in range(4):
                    for bc in range(2):
                        r = 16 * (8 * bh + 2 * bx + bc)
                        by = 2 * bh + i
                        rel = lax.rem(c + bc, 2)
                        kx, ky = order(bx, x), order(by, y)
                        gj[0, rel, kx, ky] = joined[r : r + 16]
                        gj[1, rel, ky, kx] = joined[r : r + 16]
        return b_part[0:RANK]

    b_part = attention()
    send(gls.at[c], gls.at[c], SEM["g0"], mate)

    near = [(xs, ys), (ys, xs)]
    lo, hi = pl.ds(0, HP), pl.ds(HP, HP)

    def index(name, h, i, count, k):
        return SEM[name] + (h * PARTS + i) * count + k

    def to_mate(h, i, k):
        rows = (pl.ds(0, 1), pl.ds(1, 2), pl.ds(3, 1))[k]
        send(sib_s.at[h, i, rows], sib_r.at[h, i, rows], index("sib", h, i, 3, k), mate)

    def from_mate(h, i, k):
        rows = (pl.ds(0, 1), pl.ds(1, 2), pl.ds(3, 1))[k]
        arrived(sib_r.at[h, i, rows], index("sib", h, i, 3, k))

    def product(i):
        for h in range(2):
            right = wf[h, 4 * i : 4 * i + 4].reshape(PART, COLS)
            out = dot(gj[h].reshape(PLANE, COLS), right, 1, 1).reshape(2, 4, 4, 16, PART)
            sib_s[h, i] = out[1].astype(BF16)
            own[h, i] = out[0]
        for h in range(2):
            to_mate(h, i, 0)
            if i > 0:
                to_mate(h, i - 1, 1)
            if i == PARTS - 1:
                to_mate(h, i, 1)
                for k in range(PARTS):
                    to_mate(h, k, 2)

    def stage_far(i):
        for h in range(2):
            from_mate(h, i, 0)
            far[h, i] = (own[h, i, 0] + sib_r[h, i, 0].astype(F32)).astype(BF16)
            send(far.at[h, i, :, :, lo], r1.at[h, i, 0], index("r1", h, i, 2, 0), near[h][0][0])
            send(far.at[h, i, :, :, hi], r1.at[h, i, 1], index("r1", h, i, 2, 1), near[h][0][2])

    def stage_near(i):
        for h in range(2):
            from_mate(h, i, 1)
            for k in range(2):
                arrived(r1.at[h, i, k], index("r1", h, i, 2, k))
                both = own[h, i, 1 + k] + sib_r[h, i, 1 + k].astype(F32)
                more = r1[h, i, k].astype(F32)
                if k == 0:
                    beside[h, i, k, :, :, 0:HP] = (both[:, :, 0:HP] + more).astype(BF16)
                    beside[h, i, k, :, :, HP:PART] = both[:, :, HP:PART].astype(BF16)
                else:
                    beside[h, i, k, :, :, 0:HP] = both[:, :, 0:HP].astype(BF16)
                    beside[h, i, k, :, :, HP:PART] = (both[:, :, HP:PART] + more).astype(BF16)
                send(beside.at[h, i, k], r2.at[h, i, k], index("r2", h, i, 2, k), near[h][0][2 * k])

    def columns(h, i):
        return slice(HALF * h + PART * i, HALF * h + PART * i + PART)

    def stage_own(i):
        for h in range(2):
            from_mate(h, i, 2)
            arrived(r2.at[h, i, 0], index("r2", h, i, 2, 0))
            arrived(r2.at[h, i, 1], index("r2", h, i, 2, 1))
            total = own[h, i, 3] + sib_r[h, i, 3].astype(F32) + r2[h, i, 0].astype(F32) + r2[h, i, 1].astype(F32)
            gn[:, columns(h, i)] += total[3]
            tot[h, i] = total[0:3].astype(BF16)
            for k, device in enumerate((near[h][1][1], near[h][1][0], near[h][1][2])):
                send(tot.at[h, i, k], r3.at[h, i, k], index("r3", h, i, 3, k), device)

    def stage_last(i):
        for h in range(2):
            for k in range(3):
                arrived(r3.at[h, i, k], index("r3", h, i, 3, k))
            more = r3[h, i].astype(F32)
            gn[:, columns(h, i)] += more[0] + more[1] + more[2]

    factor = float(SEQ * 32) ** (-0.5)

    def spread(ref, slot, name, devices):
        for d in range(3):
            send(ref.at[slot], ref.at[slot], SEM[name] + d, devices[d])

    def gathered(ref, slot, name):
        for d in range(3):
            arrived(ref.at[lax.rem(slot + 3 - d, 4)], SEM[name] + d)

    def small(step):
        if step == 0:
            arrived(gls.at[other_c], SEM["g0"])
            glx[x] = gls[0] + gls[1]
            spread(glx, x, "g1", xs)
        if step == 1:
            gathered(glx, x, "g1")
            gly[y] = glx[0] + glx[1] + glx[2] + glx[3]
            spread(gly, y, "g2", ys)
        if step == 2:
            gathered(gly, y, "g2")
            low = gly[0] + gly[1] + gly[2] + gly[3]
            low = jnp.concatenate([low, jnp.zeros((8, PLANE), F32)], axis=0).astype(BF16)
            token = lax.broadcasted_iota(jnp.int32, (16, PLANE), 0) + (yl * SEQ + tt * 16)
            column = lax.broadcasted_iota(jnp.int32, (16, PLANE), 1)
            pick = jnp.where(token == column, 1.0, 0.0).astype(BF16)
            gn[...] = dot(dot(pick, low, 1, 1).astype(BF16), dpad[...])
            lanes = pl.ds(pl.multiple_of(384 * (4 * y + x), 128), 384)
            a_part = dot(low, norm[:, :, :, :, :, lanes].reshape(PLANE, 384))[0:RANK]
            z1[zl, 0:RANK] = a_part
            z1[zl, RANK : 2 * RANK] = b_part
            spread(z1, zl, "z1", zq)
        if step == 3:
            gathered(z1, zl, "z1")
            z2[zh] = z1[0] + z1[1] + z1[2] + z1[3]
            spread(z2, zh, "z2", zs)
        if step == 4:
            gathered(z2, zh, "z2")
            total = (z2[0] + z2[1] + z2[2] + z2[3]) * factor
            ga[y, x] = total[0:RANK]
            gb[yl] = total[RANK : 2 * RANK]
            send(gb.at[yl], gb.at[yl], SEM["by"], pair)
            for k, device in enumerate(across):
                send(ga.at[y, x], ga.at[y, x], SEM["ax"] + k, device)
        if step == 5:
            arrived(gb.at[other_y], SEM["by"])
            for h in range(2):
                for j in range(3):
                    o_b[:, 256 * j + 128 * h : 256 * j + 128 * h + 128] = gb[h, :, 128 * j : 128 * j + 128]
            for k, (a, b) in enumerate(plane):
                arrived(ga.at[lax.rem(y + 4 - a, 4), lax.rem(x + 4 - b, 4)], SEM["ax"] + k)
            for a in range(4):
                for b in range(4):
                    k = 384 * (4 * a + b)
                    o_a[:, k : k + 384] = ga[a, b]

    product(0)
    product(1)
    stage_far(0)
    small(0)
    product(2)
    stage_far(1)
    product(3)
    stage_far(2)
    stage_far(3)
    small(1)
    for i in range(PARTS):
        stage_near(i)
    flush(40)
    small(2)
    stage_own(0)
    small(3)
    stage_own(1)
    stage_last(0)
    small(4)
    flush(34)
    stage_own(2)
    stage_last(1)
    flush(24)
    stage_own(3)
    stage_last(2)
    flush(12)
    small(5)
    stage_last(3)

    def finish():
        get_og.wait()
        gradient = gn[...] * gain[...]
        out = norm_backward(gradient, xhat[...], inv[:, 0:1])
        o_tok[...] = (og[...].astype(F32) + out).astype(BF16)

    finish()
    flush()


def copies(a, b, d, o_a, o_b, o_d):
    o_a[...] = a[...]
    o_b[...] = b[...]
    o_d[...] = d[...]


def per_device(tokens, gain, weight, down, up, out_gradient, att_gradient):
    vmem = pl.BlockSpec(memory_space=pltpu.VMEM)
    shapes = [
        ((16, WIDTH), BF16),
        ((1, WIDTH), F32),
        ((RANK, WIDTH), BF16),
        ((RANK, 2 * COLS), BF16),
        ((16, WIDTH), BF16),
        ((2, 2, 4, 2, 16, WIDTH), BF16),
        ((2, NZ, ROWS, COLS), BF16),
        ((PLANE, COLS), F32),
        ((2, SEQ, HEAD), BF16),
        ((16, WIDTH), F32),
        ((16, HEAD), F32),
        ((16, WIDTH), BF16),
        ((16, COLS), BF16),
        ((PLANE, 16), BF16),
        ((2, 2, 4, 4, 16, COLS), BF16),
        ((2, PARTS, 4, 4, 16, PART), BF16),
        ((2, PARTS, 4, 4, 16, PART), BF16),
        ((2, PARTS, 4, 4, 16, PART), F32),
        ((2, PARTS, 4, 16, PART), BF16),
        ((2, PARTS, 2, 4, 16, HP), BF16),
        ((2, PARTS, 2, 4, 16, PART), BF16),
        ((2, PARTS, 2, 4, 16, PART), BF16),
        ((2, PARTS, 3, 16, PART), BF16),
        ((2, PARTS, 3, 16, PART), BF16),
        ((16, WIDTH), F32),
        ((2, RANK, PLANE), F32),
        ((4, RANK, PLANE), F32),
        ((4, RANK, PLANE), F32),
        ((4, 2 * RANK, COLS), F32),
        ((4, 2 * RANK, COLS), F32),
        ((4, 4, RANK, 384), F32),
        ((2, RANK, COLS), F32),
    ]
    scratch = [pltpu.VMEM(shape, kind) for shape, kind in shapes]
    scratch += [pltpu.SemaphoreType.DMA((N_SEM,)), pltpu.SemaphoreType.DMA((N_SEM,)), pltpu.SemaphoreType.DMA((9,))]
    out_shape = (
        jax.ShapeDtypeStruct((16, WIDTH), BF16),
        jax.ShapeDtypeStruct((RANK, WIDTH), F32),
        jax.ShapeDtypeStruct((RANK, 2 * COLS), F32),
    )
    results = pl.pallas_call(
        kernel,
        out_shape=out_shape,
        in_specs=[pl.BlockSpec(memory_space=pltpu.HBM)] * 7,
        out_specs=(vmem, vmem, vmem),
        scratch_shapes=scratch,
        compiler_params=pltpu.CompilerParams(
            collective_id=0, has_side_effects=True, vmem_limit_bytes=60 * 1024 * 1024
        ),
    )(tokens, gain.reshape(1, WIDTH), weight, down, up, out_gradient, att_gradient)
    return pl.pallas_call(
        copies,
        out_shape=out_shape,
        in_specs=[vmem] * 3,
        out_specs=(vmem, vmem, vmem),
    )(*results)


def solution(mesh):
    placed = (
        P(("dp", "tensor"), None),
        P(),
        P("dp", "tensor"),
        P(),
        P(None, "tensor"),
        P(("dp", "tensor"), None),
        P("dp", "tensor"),
    )
    return jax.shard_map(
        per_device,
        mesh=mesh,
        in_specs=placed,
        out_specs=(P(("dp", "tensor"), None), P(), P(None, "tensor")),
        check_vma=False,
    )
```

```python
import jax
import jax.numpy as jnp
from jax import lax
from jax.experimental import pallas as pl
from jax.experimental.pallas import tpu as pltpu
from jax.sharding import PartitionSpec as P

HEAD = 128
SEQ = 256
WIDTH = 6144
HALF = WIDTH // 2
RANK = 8
NZ = 16
ROWS = 192
COLS = 3 * HEAD
PARTS = 4
PART = HALF // PARTS
HP = PART // 2
PLANE = 512
EPSILON = 1e-06
F32 = jnp.float32
BF16 = jnp.bfloat16


def row_norm(values):
    mean = jnp.mean(values, axis=-1, keepdims=True)
    centred = values - mean
    inverse = lax.rsqrt(jnp.mean(centred * centred, axis=-1, keepdims=True) + EPSILON)
    return centred * inverse, inverse


def norm_backward(gradient, normal, inverse):
    return (
        gradient
        - jnp.mean(gradient, axis=-1, keepdims=True)
        - normal * jnp.mean(gradient * normal, axis=-1, keepdims=True)
    ) * inverse


def dot(a, b, ca=1, cb=0):
    return lax.dot_general(a, b, (((ca,), (cb,)), ((), ())), preferred_element_type=F32)


class Allocator:
    def __init__(self):
        self.size = 0

    def take(self, count):
        base = self.size
        self.size += count
        return base


def plan():
    al = Allocator()
    names = dict(
        wy=6, do=1, ring=64, t1=6, t2=6, t3=2,
        sib=4 * PARTS, r1=4 * PARTS, r2=4 * PARTS, r3=6 * PARTS,
        g0=1, g1=3, g2=3, z1=3, z2=3, ax=15, by=1,
    )
    bases = {name: al.take(count) for name, count in names.items()}
    return bases, al.size


SEM, N_SEM = plan()


def kernel(
    tok_in, gain_in, w_in, down_in, up_in, og_in, dout_in,
    o_tok, o_a, o_b,
    tok, gain, down, up, og,
    norm, wf, acc, dall, xhat, inv, dpad, upad, lowr,
    gj, sib_s, sib_r, own, far, r1, beside, r2, tot, r3, gn,
    gls, glx, gly, z1, z2, ga, gb,
    ssem, rsem, lsem,
):
    dp = lax.axis_index("dp")
    tt = lax.axis_index("tensor")
    yl, z = lax.div(dp, NZ), lax.rem(dp, NZ)
    yh = lax.div(tt, 8)
    x = lax.rem(lax.div(tt, 2), 4)
    c = lax.rem(tt, 2)
    y = 2 * yh + yl
    zh, zl = lax.div(z, 4), lax.rem(z, 4)
    other_c = 1 - c
    other_y = 1 - yl

    def at(y_, x_, z_, c_):
        return (
            lax.rem(y_, 2) * NZ + z_,
            lax.div(y_, 2) * 8 + x_ * 2 + c_,
        )

    xs = [at(y, lax.rem(x + d, 4), z, c) for d in (1, 2, 3)]
    ys = [at(lax.rem(y + d, 4), x, z, c) for d in (1, 2, 3)]
    zu = at(y, x, lax.rem(z + 1, NZ), c)
    zd = at(y, x, lax.rem(z + NZ - 1, NZ), c)
    zq = [at(y, x, zh * 4 + lax.rem(zl + d, 4), c) for d in (1, 2, 3)]
    zs = [at(y, x, lax.rem(zh + d, 4) * 4 + zl, c) for d in (1, 2, 3)]
    mate = at(y, x, z, other_c)
    pair = at(2 * yh + other_y, x, z, c)
    plane = [(a, b) for a in range(4) for b in range(4) if a + b > 0]
    across = [at(lax.rem(y + a, 4), lax.rem(x + b, 4), z, c) for a, b in plane]
    peers = [mate, *across, zu, zd]
    later_peers = [*zq, *zs]

    def copy(src, dst, k, device):
        return pltpu.make_async_remote_copy(
            src_ref=src, dst_ref=dst, send_sem=ssem.at[k], recv_sem=rsem.at[k],
            device_id=device, device_id_type=pl.DeviceIdType.MESH,
        )

    pending = []

    def send(src, dst, k, device):
        one = copy(src, dst, k, device)
        one.start()
        pending.append(one)

    def arrived(ref, k):
        copy(ref, ref, k, mate).wait_recv()

    def flush(keep=0):
        while len(pending) > keep:
            pending.pop(0).wait_send()

    barrier = pltpu.get_barrier_semaphore()
    for device in peers:
        pl.semaphore_signal(barrier, inc=1, device_id=device, device_id_type=pl.DeviceIdType.MESH)

    own_cols = pl.ds(pl.multiple_of(yl * HEAD, HEAD), HEAD)
    pair_cols = pl.ds(pl.multiple_of(other_y * HEAD, HEAD), HEAD)
    locals_ = []

    def fetch(src, dst):
        one = pltpu.make_async_copy(src, dst, lsem.at[len(locals_)])
        one.start()
        locals_.append(one)
        return one

    get_w = []
    for j in range(3):
        cols = pl.ds(pl.multiple_of(256 * j + yl * HEAD, HEAD), HEAD)
        get_w.append(fetch(w_in.at[:, cols], wf.at[yl, z, :, pl.ds(128 * j, 128)]))
    get_tok = [fetch(tok_in, tok), fetch(gain_in, gain)]
    get_small = [fetch(down_in, down), fetch(up_in, up), fetch(dout_in.at[:, own_cols], dall.at[yl])]
    get_og = fetch(og_in, og)

    pl.semaphore_wait(barrier, len(peers))

    rows_of = (pl.ds(0, ROWS // 2), pl.ds(ROWS // 2, ROWS // 2))
    for k in range(2):
        for j in range(3):
            cols = pl.ds(pl.multiple_of(256 * j + other_y * HEAD, HEAD), HEAD)
            to = wf.at[yl, z, rows_of[k], pl.ds(128 * j, 128)]
            send(w_in.at[rows_of[k], cols], to, SEM["wy"] + 3 * k + j, pair)
    for one in get_w:
        one.wait()

    def ring_index(way, step, j, k):
        return SEM["ring"] + way * 32 + (step - 1) * 4 + 2 * j + k

    def ring_send(way, step, j, k):
        block = lax.rem(z + NZ - (step - 1), NZ) if way == 0 else lax.rem(z + step - 1, NZ)
        ref = wf.at[j, block, rows_of[k]]
        send(ref, ref, ring_index(way, step, j, k), zu if way == 0 else zd)

    def ring_wait(way, step, j, k):
        block = lax.rem(z + NZ - step, NZ) if way == 0 else lax.rem(z + step, NZ)
        arrived(wf.at[j, block, rows_of[k]], ring_index(way, step, j, k))

    for k in range(2):
        for way in range(2):
            ring_send(way, 1, yl, k)
    for one in get_tok:
        one.wait()
    normal, inverse = row_norm(tok[...].astype(F32))
    xhat[...] = normal
    inv[...] = jnp.broadcast_to(inverse, inv.shape)
    norm[yl, yh, x, c] = (normal * gain[...]).astype(BF16)

    a_cols, b_cols = pl.ds(0, HALF), pl.ds(HALF, HALF)
    a_ref = norm.at[yl, yh, x, c, :, a_cols]
    b_ref = norm.at[yl, yh, x, c, :, b_cols]
    for d in range(3):
        send(a_ref, a_ref, SEM["t1"] + d, xs[d])
        send(b_ref, b_ref, SEM["t1"] + 3 + d, ys[d])
    send(dout_in.at[:, pair_cols], dall.at[yl], SEM["do"], pair)
    for one in get_small:
        one.wait()

    dpad[...] = jnp.concatenate([down[...].astype(F32), jnp.zeros((8, WIDTH), F32)], axis=0).astype(BF16)
    for j in range(3):
        cols = pl.ds(pl.multiple_of(256 * j + yl * HEAD, HEAD), HEAD)
        upad[:, 128 * j : 128 * j + 128] = jnp.concatenate(
            [up[:, cols].astype(F32), jnp.zeros((8, HEAD), F32)], axis=0
        ).astype(BF16)

    for k in range(2):
        for way in range(2):
            ring_wait(way, 1, yl, k)
            ring_send(way, 2, yl, k)
        for j in range(3):
            arrived(wf.at[other_y, z, rows_of[k], pl.ds(128 * j, 128)], SEM["wy"] + 3 * k + j)
        for way in range(2):
            ring_send(way, 1, other_y, k)

    def forward(step):
        up_way = lax.rem(step + z, 2)
        base = lax.rem(up_way * (z + step - 1) + (1 - up_way) * (z - step + NZ), NZ)
        block = lax.div(base, 2)
        for j in range(2):
            lanes = pl.ds(pl.multiple_of(HALF * j + 2 * ROWS * block, 128), 2 * ROWS)
            left = norm[:, :, :, :, :, lanes].reshape(PLANE, 2 * ROWS)
            right = wf[j, pl.ds(2 * block, 2)].reshape(2 * ROWS, COLS)
            acc[...] += dot(left, right)

    def tokens_second():
        for d in range(3):
            xd, yd = lax.rem(x + 3 - d, 4), lax.rem(y + 3 - d, 4)
            arrived(norm.at[yl, yh, xd, c, :, a_cols], SEM["t1"] + d)
            arrived(norm.at[lax.rem(yd, 2), lax.div(yd, 2), x, c, :, b_cols], SEM["t1"] + 3 + d)
        ra = norm.at[yl, yh, :, c, :, a_cols]
        rb = norm.at[:, :, x, c, :, b_cols]
        for d in range(3):
            send(ra, ra, SEM["t2"] + d, ys[d])
            send(rb, rb, SEM["t2"] + 3 + d, xs[d])

    def tokens_mate():
        for d in range(3):
            yd = lax.rem(y + 3 - d, 4)
            arrived(norm.at[lax.rem(yd, 2), lax.div(yd, 2), :, c, :, a_cols], SEM["t2"] + d)
        ref = norm.at[:, :, :, c, :, a_cols]
        send(ref, ref, SEM["t3"], mate)
        for d in range(3):
            xd = lax.rem(x + 3 - d, 4)
            arrived(norm.at[:, :, xd, c, :, b_cols], SEM["t2"] + 3 + d)
        ref = norm.at[:, :, :, c, :, b_cols]
        send(ref, ref, SEM["t3"] + 1, mate)

    def tokens_done():
        arrived(norm.at[:, :, :, other_c, :, a_cols], SEM["t3"])
        arrived(norm.at[:, :, :, other_c, :, b_cols], SEM["t3"] + 1)

    def forward_first():
        low = dot(norm[...].reshape(PLANE, WIDTH), dpad[...], 1, 1).astype(BF16)
        lowr[...] = low
        acc[...] = dot(low, upad[...])

        def several(s, carry):
            forward(s)
            return carry

        lax.fori_loop(1, 6, several, 0)

    def ring_step(step):
        if step < 8:
            for j in (yl, other_y) if step > 2 else (other_y,):
                for k in range(2):
                    for way in range(2):
                        ring_wait(way, step - 1, j, k)
                        ring_send(way, step, j, k)
        elif step == 8:
            for k in range(2):
                for way in range(2):
                    ring_wait(way, 7, way, k)
                    ring_send(way, 8, way, k)
            for k in range(2):
                for way in range(2):
                    ring_wait(way, 7, 1 - way, k)
        else:
            for k in range(2):
                for way in range(2):
                    ring_wait(way, 8, way, k)

    def dout_done():
        arrived(dall.at[other_y], SEM["do"])
        flush(8)

    for step in range(2, 10):
        ring_step(step)
        if step == 2:
            tokens_second()
        if step == 6:
            tokens_mate()
        if step == 7:
            tokens_done()
            forward_first()
        if step == 8:
            forward(6)
            forward(7)
            dout_done()
        if step == 9:
            forward(8)

    for device in later_peers:
        pl.semaphore_signal(barrier, inc=1, device_id=device, device_id_type=pl.DeviceIdType.MESH)

    def order(to, me):
        d = lax.rem(to - me + 6, 4)
        return lax.rem(2 * d, 5) - lax.div(d, 2) * (1 - lax.div(d, 3))

    scale = HEAD ** (-0.5)
    def attention():
        for i in range(2):
            rows = slice(SEQ * i, SEQ * i + SEQ)
            q_norm, q_inv = row_norm(acc[rows, 0:128])
            k_norm, k_inv = row_norm(acc[rows, 128:256])
            value = acc[rows, 256:384].astype(BF16)
            query, key = q_norm.astype(BF16), k_norm.astype(BF16)
            weights = jnp.exp(dot(query, key, 1, 1) * scale)
            probs = weights / jnp.sum(weights, axis=-1, keepdims=True)
            cot = dall[i]
            g_value = dot(probs.astype(BF16), cot, 0, 0)
            g_probs = dot(cot, value, 1, 1)
            g_scores = probs * (g_probs - jnp.sum(probs * g_probs, axis=-1, keepdims=True))
            g_scores = (g_scores * scale).astype(BF16)
            g_query = norm_backward(dot(g_scores, key), q_norm, q_inv)
            g_key = norm_backward(dot(g_scores, query, 0, 0), k_norm, k_inv)
            joined = jnp.concatenate([g_query, g_key, g_value], axis=1).astype(BF16)
            gls[c, :, SEQ * i : SEQ * i + SEQ] = dot(upad[...], joined, 1, 1)[0:RANK]
            if i == 0:
                b_part = dot(lowr[rows], joined, 0, 0)
            else:
                b_part = b_part + dot(lowr[rows], joined, 0, 0)
            for bh in range(2):
                for bx in range(4):
                    for bc in range(2):
                        r = 16 * (8 * bh + 2 * bx + bc)
                        by = 2 * bh + i
                        rel = lax.rem(c + bc, 2)
                        kx, ky = order(bx, x), order(by, y)
                        gj[0, rel, kx, ky] = joined[r : r + 16]
                        gj[1, rel, ky, kx] = joined[r : r + 16]
        return b_part[0:RANK]

    b_part = attention()
    send(gls.at[c], gls.at[c], SEM["g0"], mate)

    near = [(xs, ys), (ys, xs)]
    lo, hi = pl.ds(0, HP), pl.ds(HP, HP)

    def index(name, h, i, count, k):
        return SEM[name] + (h * PARTS + i) * count + k

    def to_mate(h, i, k):
        rows = (pl.ds(0, 1), pl.ds(1, 3))[k]
        send(sib_s.at[h, i, rows], sib_r.at[h, i, rows], index("sib", h, i, 2, k), mate)

    def from_mate(h, i, k):
        rows = (pl.ds(0, 1), pl.ds(1, 3))[k]
        arrived(sib_r.at[h, i, rows], index("sib", h, i, 2, k))

    def product(i):
        for h in range(2):
            right = wf[h, 4 * i : 4 * i + 4].reshape(PART, COLS)
            out = dot(gj[h].reshape(PLANE, COLS), right, 1, 1).reshape(2, 4, 4, 16, PART)
            sib_s[h, i] = out[1].astype(BF16)
            own[h, i] = out[0]
        for h in range(2):
            to_mate(h, i, 0)
            if i > 0:
                to_mate(h, i - 1, 1)
            if i == PARTS - 1:
                to_mate(h, i, 1)

    def stage_far(i):
        for h in range(2):
            from_mate(h, i, 0)
            far[h, i] = (own[h, i, 0] + sib_r[h, i, 0].astype(F32)).astype(BF16)
            send(far.at[h, i, :, :, lo], r1.at[h, i, 0], index("r1", h, i, 2, 0), near[h][0][0])
            send(far.at[h, i, :, :, hi], r1.at[h, i, 1], index("r1", h, i, 2, 1), near[h][0][2])

    def stage_near(i):
        for h in range(2):
            from_mate(h, i, 1)
            for k in range(2):
                arrived(r1.at[h, i, k], index("r1", h, i, 2, k))
                both = own[h, i, 1 + k] + sib_r[h, i, 1 + k].astype(F32)
                more = r1[h, i, k].astype(F32)
                if k == 0:
                    beside[h, i, k, :, :, 0:HP] = (both[:, :, 0:HP] + more).astype(BF16)
                    beside[h, i, k, :, :, HP:PART] = both[:, :, HP:PART].astype(BF16)
                else:
                    beside[h, i, k, :, :, 0:HP] = both[:, :, 0:HP].astype(BF16)
                    beside[h, i, k, :, :, HP:PART] = (both[:, :, HP:PART] + more).astype(BF16)
                send(beside.at[h, i, k], r2.at[h, i, k], index("r2", h, i, 2, k), near[h][0][2 * k])

    def columns(h, i):
        return slice(HALF * h + PART * i, HALF * h + PART * i + PART)

    def stage_own(i):
        for h in range(2):
            arrived(r2.at[h, i, 0], index("r2", h, i, 2, 0))
            arrived(r2.at[h, i, 1], index("r2", h, i, 2, 1))
            total = own[h, i, 3] + sib_r[h, i, 3].astype(F32) + r2[h, i, 0].astype(F32) + r2[h, i, 1].astype(F32)
            gn[:, columns(h, i)] += total[3]
            tot[h, i] = total[0:3].astype(BF16)
            for k, device in enumerate((near[h][1][1], near[h][1][0], near[h][1][2])):
                send(tot.at[h, i, k], r3.at[h, i, k], index("r3", h, i, 3, k), device)

    sums = [0.0, 0.0]

    def stage_last(i):
        for h in range(2):
            for k in range(3):
                arrived(r3.at[h, i, k], index("r3", h, i, 3, k))
            more = r3[h, i].astype(F32)
            cols = columns(h, i)
            grad = (gn[:, cols] + (more[0] + more[1] + more[2])) * gain[:, cols]
            gn[:, cols] = grad
            sums[0] += jnp.sum(grad, axis=-1, keepdims=True)
            sums[1] += jnp.sum(grad * xhat[:, cols], axis=-1, keepdims=True)

    factor = float(SEQ * 32) ** (-0.5)

    def spread(ref, slot, name, devices):
        for d in range(3):
            send(ref.at[slot], ref.at[slot], SEM[name] + d, devices[d])

    def gathered(ref, slot, name):
        for d in range(3):
            arrived(ref.at[lax.rem(slot + 3 - d, 4)], SEM[name] + d)

    def small(step):
        if step == 0:
            arrived(gls.at[other_c], SEM["g0"])
            glx[x] = gls[0] + gls[1]
            spread(glx, x, "g1", xs)
        if step == 1:
            gathered(glx, x, "g1")
            gly[y] = glx[0] + glx[1] + glx[2] + glx[3]
            spread(gly, y, "g2", ys)
        if step == 2:
            gathered(gly, y, "g2")
            low = gly[0] + gly[1] + gly[2] + gly[3]
            low = jnp.concatenate([low, jnp.zeros((8, PLANE), F32)], axis=0).astype(BF16)
            token = lax.broadcasted_iota(jnp.int32, (16, PLANE), 0) + (yl * SEQ + tt * 16)
            column = lax.broadcasted_iota(jnp.int32, (16, PLANE), 1)
            pick = jnp.where(token == column, 1.0, 0.0).astype(BF16)
            gn[...] = dot(dot(pick, low, 1, 1).astype(BF16), dpad[...])
            lanes = pl.ds(pl.multiple_of(384 * (4 * y + x), 128), 384)
            a_part = dot(low, norm[:, :, :, :, :, lanes].reshape(PLANE, 384))[0:RANK]
            z1[zl, 0:RANK] = a_part
            z1[zl, RANK : 2 * RANK] = b_part
            pl.semaphore_wait(barrier, len(later_peers))
            spread(z1, zl, "z1", zq)
        if step == 3:
            gathered(z1, zl, "z1")
            z2[zh] = z1[0] + z1[1] + z1[2] + z1[3]
            spread(z2, zh, "z2", zs)
        if step == 4:
            gathered(z2, zh, "z2")
            total = (z2[0] + z2[1] + z2[2] + z2[3]) * factor
            ga[y, x] = total[0:RANK]
            gb[yl] = total[RANK : 2 * RANK]
            send(gb.at[yl], gb.at[yl], SEM["by"], pair)
            for k, device in enumerate(across):
                send(ga.at[y, x], ga.at[y, x], SEM["ax"] + k, device)
        if step == 5:
            arrived(gb.at[other_y], SEM["by"])
            for h in range(2):
                for j in range(3):
                    o_b[:, 256 * j + 128 * h : 256 * j + 128 * h + 128] = gb[h, :, 128 * j : 128 * j + 128]
            for k, (a, b) in enumerate(plane):
                arrived(ga.at[lax.rem(y + 4 - a, 4), lax.rem(x + 4 - b, 4)], SEM["ax"] + k)
            for a in range(4):
                for b in range(4):
                    k = 384 * (4 * a + b)
                    o_a[:, k : k + 384] = ga[a, b]

    product(0)
    product(1)
    stage_far(0)
    small(0)
    product(2)
    stage_far(1)
    product(3)
    stage_far(2)
    stage_far(3)
    small(1)
    for i in range(PARTS):
        stage_near(i)
    flush(40)
    small(2)
    stage_own(0)
    small(3)
    stage_own(1)
    stage_own(2)
    small(4)
    stage_own(3)
    flush(54)
    stage_last(0)
    stage_last(1)
    small(5)
    flush(24)
    stage_last(2)
    stage_last(3)

    def finish():
        get_og.wait()
        first, second = sums[0] * (1.0 / WIDTH), sums[1] * (1.0 / WIDTH)
        out = (gn[...] - first - xhat[...] * second) * inv[:, 0:1]
        o_tok[...] = (og[...].astype(F32) + out).astype(BF16)

    finish()
    flush()


def copies(a, b, d, o_a, o_b, o_d):
    o_a[...] = a[...]
    o_b[...] = b[...]
    o_d[...] = d[...]


def per_device(tokens, gain, weight, down, up, out_gradient, att_gradient):
    vmem = pl.BlockSpec(memory_space=pltpu.VMEM)
    hbm = pl.BlockSpec(memory_space=pltpu.HBM)
    shapes = [
        ((16, WIDTH), BF16),
        ((1, WIDTH), F32),
        ((RANK, WIDTH), BF16),
        ((RANK, 2 * COLS), BF16),
        ((16, WIDTH), BF16),
        ((2, 2, 4, 2, 16, WIDTH), BF16),
        ((2, NZ, ROWS, COLS), BF16),
        ((PLANE, COLS), F32),
        ((2, SEQ, HEAD), BF16),
        ((16, WIDTH), F32),
        ((16, HEAD), F32),
        ((16, WIDTH), BF16),
        ((16, COLS), BF16),
        ((PLANE, 16), BF16),
        ((2, 2, 4, 4, 16, COLS), BF16),
        ((2, PARTS, 4, 4, 16, PART), BF16),
        ((2, PARTS, 4, 4, 16, PART), BF16),
        ((2, PARTS, 4, 4, 16, PART), F32),
        ((2, PARTS, 4, 16, PART), BF16),
        ((2, PARTS, 2, 4, 16, HP), BF16),
        ((2, PARTS, 2, 4, 16, PART), BF16),
        ((2, PARTS, 2, 4, 16, PART), BF16),
        ((2, PARTS, 3, 16, PART), BF16),
        ((2, PARTS, 3, 16, PART), BF16),
        ((16, WIDTH), F32),
        ((2, RANK, PLANE), F32),
        ((4, RANK, PLANE), F32),
        ((4, RANK, PLANE), F32),
        ((4, 2 * RANK, COLS), F32),
        ((4, 2 * RANK, COLS), F32),
        ((4, 4, RANK, 384), F32),
        ((2, RANK, COLS), F32),
    ]
    scratch = [pltpu.VMEM(shape, kind) for shape, kind in shapes]
    scratch += [pltpu.SemaphoreType.DMA((N_SEM,)), pltpu.SemaphoreType.DMA((N_SEM,)), pltpu.SemaphoreType.DMA((9,))]
    out_shape = (
        jax.ShapeDtypeStruct((16, WIDTH), BF16),
        jax.ShapeDtypeStruct((RANK, WIDTH), F32),
        jax.ShapeDtypeStruct((RANK, 2 * COLS), F32),
    )
    results = pl.pallas_call(
        kernel,
        out_shape=out_shape,
        in_specs=[hbm] * 7,
        out_specs=(vmem, vmem, vmem),
        scratch_shapes=scratch,
        compiler_params=pltpu.CompilerParams(
            collective_id=0, has_side_effects=True, vmem_limit_bytes=60 * 1024 * 1024
        ),
    )(tokens, gain.reshape(1, WIDTH), weight, down, up, out_gradient, att_gradient)
    return pl.pallas_call(
        copies,
        out_shape=out_shape,
        in_specs=[vmem] * 3,
        out_specs=(vmem, vmem, vmem),
    )(*results)


def solution(mesh):
    placed = (
        P(("dp", "tensor"), None),
        P(),
        P("dp", "tensor"),
        P(),
        P(None, "tensor"),
        P(("dp", "tensor"), None),
        P("dp", "tensor"),
    )
    return jax.shard_map(
        per_device,
        mesh=mesh,
        in_specs=placed,
        out_specs=(P(("dp", "tensor"), None), P(), P(None, "tensor")),
        check_vma=False,
    )
```

```python
import jax
import jax.numpy as jnp
from jax import lax
from jax.experimental import pallas as pl
from jax.experimental.pallas import tpu as pltpu
from jax.sharding import PartitionSpec as P

HEAD = 128
SEQ = 256
WIDTH = 6144
HALF = WIDTH // 2
RANK = 8
NZ = 16
ROWS = 192
COLS = 3 * HEAD
PIECES = 1
PARTS = 4
PART = HALF // PARTS
HP = PART // 2
PLANE = 512
EPSILON = 1e-06
F32 = jnp.float32
BF16 = jnp.bfloat16


def row_norm(values):
    mean = jnp.mean(values, axis=-1, keepdims=True)
    centred = values - mean
    inverse = lax.rsqrt(jnp.mean(centred * centred, axis=-1, keepdims=True) + EPSILON)
    return centred * inverse, inverse


def norm_backward(gradient, normal, inverse):
    return (
        gradient
        - jnp.mean(gradient, axis=-1, keepdims=True)
        - normal * jnp.mean(gradient * normal, axis=-1, keepdims=True)
    ) * inverse


def dot(a, b, ca=1, cb=0):
    return lax.dot_general(a, b, (((ca,), (cb,)), ((), ())), preferred_element_type=F32)


class Allocator:
    def __init__(self):
        self.size = 0

    def take(self, count):
        base = self.size
        self.size += count
        return base


def plan():
    al = Allocator()
    names = dict(
        wy=6, do=1, ring=64, t1=6, t2=6, t3=2,
        sib=4 * PARTS, r1=4 * PARTS, r2=4 * PARTS, r3=6 * PARTS,
        g0=1, g1=3, g2=3, z1=3, z2=3, ax=15, by=1,
    )
    bases = {name: al.take(count) for name, count in names.items()}
    return bases, al.size


SEM, N_SEM = plan()


def kernel(
    tok_in, gain_in, w_in, down_in, up_in, og_in, dout_in,
    o_tok, o_a, o_b,
    tok, gain, down, up, og,
    norm, wf, acc, dall, xhat, inv, dpad, upad, lowr,
    gj, sib_s, sib_r, own, far, r1, beside, r2, tot, r3, gn,
    gls, glx, gly, z1, z2, ga, gb,
    ssem, rsem, lsem,
):
    dp = lax.axis_index("dp")
    tt = lax.axis_index("tensor")
    yl, z = lax.div(dp, NZ), lax.rem(dp, NZ)
    yh = lax.div(tt, 8)
    x = lax.rem(lax.div(tt, 2), 4)
    c = lax.rem(tt, 2)
    y = 2 * yh + yl
    zh, zl = lax.div(z, 4), lax.rem(z, 4)
    other_c = 1 - c
    other_y = 1 - yl

    def at(y_, x_, z_, c_):
        return (
            lax.rem(y_, 2) * NZ + z_,
            lax.div(y_, 2) * 8 + x_ * 2 + c_,
        )

    xs = [at(y, lax.rem(x + d, 4), z, c) for d in (1, 2, 3)]
    ys = [at(lax.rem(y + d, 4), x, z, c) for d in (1, 2, 3)]
    zu = at(y, x, lax.rem(z + 1, NZ), c)
    zd = at(y, x, lax.rem(z + NZ - 1, NZ), c)
    zq = [at(y, x, zh * 4 + lax.rem(zl + d, 4), c) for d in (1, 2, 3)]
    zs = [at(y, x, lax.rem(zh + d, 4) * 4 + zl, c) for d in (1, 2, 3)]
    mate = at(y, x, z, other_c)
    pair = at(2 * yh + other_y, x, z, c)
    plane = [(a, b) for a in range(4) for b in range(4) if a + b > 0]
    across = [at(lax.rem(y + a, 4), lax.rem(x + b, 4), z, c) for a, b in plane]
    peers = [mate, *across, zu, zd]
    later_peers = [*zq, *zs]

    def copy(src, dst, k, device):
        return pltpu.make_async_remote_copy(
            src_ref=src, dst_ref=dst, send_sem=ssem.at[k], recv_sem=rsem.at[k],
            device_id=device, device_id_type=pl.DeviceIdType.MESH,
        )

    pending = []

    def send(src, dst, k, device):
        one = copy(src, dst, k, device)
        one.start()
        pending.append(one)

    def arrived(ref, k):
        copy(ref, ref, k, mate).wait_recv()

    def flush(keep=0):
        while len(pending) > keep:
            pending.pop(0).wait_send()

    barrier = pltpu.get_barrier_semaphore()
    for device in peers:
        pl.semaphore_signal(barrier, inc=1, device_id=device, device_id_type=pl.DeviceIdType.MESH)

    own_cols = pl.ds(pl.multiple_of(yl * HEAD, HEAD), HEAD)
    pair_cols = pl.ds(pl.multiple_of(other_y * HEAD, HEAD), HEAD)
    locals_ = []

    def fetch(src, dst):
        one = pltpu.make_async_copy(src, dst, lsem.at[len(locals_)])
        one.start()
        locals_.append(one)
        return one

    get_w = []
    for j in range(3):
        cols = pl.ds(pl.multiple_of(256 * j + yl * HEAD, HEAD), HEAD)
        get_w.append(fetch(w_in.at[:, cols], wf.at[yl, z, :, pl.ds(128 * j, 128)]))
    get_tok = [fetch(tok_in, tok), fetch(gain_in, gain)]
    get_small = [fetch(down_in, down), fetch(up_in, up), fetch(dout_in.at[:, own_cols], dall.at[yl])]
    get_og = fetch(og_in, og)

    for one in get_tok:
        one.wait()
    normal, inverse = row_norm(tok[...].astype(F32))
    xhat[...] = normal
    inv[...] = jnp.broadcast_to(inverse, inv.shape)
    norm[yl, yh, x, c] = (normal * gain[...]).astype(BF16)

    for one in get_small:
        one.wait()

    dpad[...] = jnp.concatenate([down[...].astype(F32), jnp.zeros((8, WIDTH), F32)], axis=0).astype(BF16)
    for j in range(3):
        cols = pl.ds(pl.multiple_of(256 * j + yl * HEAD, HEAD), HEAD)
        upad[:, 128 * j : 128 * j + 128] = jnp.concatenate(
            [up[:, cols].astype(F32), jnp.zeros((8, HEAD), F32)], axis=0
        ).astype(BF16)

    pl.semaphore_wait(barrier, len(peers))

    piece = ROWS // PIECES
    rows_of = [pl.ds(piece * k, piece) for k in range(PIECES)]
    for k in range(PIECES):
        for j in range(3):
            cols = pl.ds(pl.multiple_of(256 * j + other_y * HEAD, HEAD), HEAD)
            to = wf.at[yl, z, rows_of[k], pl.ds(128 * j, 128)]
            send(w_in.at[rows_of[k], cols], to, SEM["wy"] + 3 * k + j, pair)
    for one in get_w:
        one.wait()

    def ring_index(way, step, j, k):
        return SEM["ring"] + way * 32 + (step - 1) * 4 + 2 * j + k

    def ring_send(way, step, j, k):
        block = lax.rem(z + NZ - (step - 1), NZ) if way == 0 else lax.rem(z + step - 1, NZ)
        ref = wf.at[j, block, rows_of[k]]
        send(ref, ref, ring_index(way, step, j, k), zu if way == 0 else zd)

    def ring_wait(way, step, j, k):
        block = lax.rem(z + NZ - step, NZ) if way == 0 else lax.rem(z + step, NZ)
        arrived(wf.at[j, block, rows_of[k]], ring_index(way, step, j, k))

    for k in range(PIECES):
        for way in range(2):
            ring_send(way, 1, yl, k)
    a_cols, b_cols = pl.ds(0, HALF), pl.ds(HALF, HALF)
    a_ref = norm.at[yl, yh, x, c, :, a_cols]
    b_ref = norm.at[yl, yh, x, c, :, b_cols]
    for d in range(3):
        send(a_ref, a_ref, SEM["t1"] + d, xs[d])
        send(b_ref, b_ref, SEM["t1"] + 3 + d, ys[d])
    send(dout_in.at[:, pair_cols], dall.at[yl], SEM["do"], pair)
    for k in range(PIECES):
        for way in range(2):
            ring_wait(way, 1, yl, k)
            ring_send(way, 2, yl, k)
        for j in range(3):
            arrived(wf.at[other_y, z, rows_of[k], pl.ds(128 * j, 128)], SEM["wy"] + 3 * k + j)
        for way in range(2):
            ring_send(way, 1, other_y, k)

    def forward(step):
        up_way = lax.rem(step + z, 2)
        base = lax.rem(up_way * (z + step - 1) + (1 - up_way) * (z - step + NZ), NZ)
        block = lax.div(base, 2)
        left = []
        for j in range(2):
            lanes = pl.ds(pl.multiple_of(HALF * j + 2 * ROWS * block, 128), 2 * ROWS)
            left.append(norm[:, :, :, :, :, lanes].reshape(PLANE, 2 * ROWS))
        right = wf[:, pl.ds(2 * block, 2)].reshape(4 * ROWS, COLS)
        acc[...] += dot(jnp.concatenate(left, axis=1), right)

    def tokens_second():
        for d in range(3):
            xd, yd = lax.rem(x + 3 - d, 4), lax.rem(y + 3 - d, 4)
            arrived(norm.at[yl, yh, xd, c, :, a_cols], SEM["t1"] + d)
            arrived(norm.at[lax.rem(yd, 2), lax.div(yd, 2), x, c, :, b_cols], SEM["t1"] + 3 + d)
        ra = norm.at[yl, yh, :, c, :, a_cols]
        rb = norm.at[:, :, x, c, :, b_cols]
        for d in range(3):
            send(ra, ra, SEM["t2"] + d, ys[d])
            send(rb, rb, SEM["t2"] + 3 + d, xs[d])

    def tokens_mate():
        for d in range(3):
            yd = lax.rem(y + 3 - d, 4)
            arrived(norm.at[lax.rem(yd, 2), lax.div(yd, 2), :, c, :, a_cols], SEM["t2"] + d)
        ref = norm.at[:, :, :, c, :, a_cols]
        send(ref, ref, SEM["t3"], mate)
        for d in range(3):
            xd = lax.rem(x + 3 - d, 4)
            arrived(norm.at[:, :, xd, c, :, b_cols], SEM["t2"] + 3 + d)
        ref = norm.at[:, :, :, c, :, b_cols]
        send(ref, ref, SEM["t3"] + 1, mate)

    def tokens_done():
        arrived(norm.at[:, :, :, other_c, :, a_cols], SEM["t3"])
        arrived(norm.at[:, :, :, other_c, :, b_cols], SEM["t3"] + 1)

    def forward_first():
        low = dot(norm[...].reshape(PLANE, WIDTH), dpad[...], 1, 1).astype(BF16)
        lowr[...] = low
        acc[...] = dot(low, upad[...])

        def several(s, carry):
            forward(s)
            return carry

        lax.fori_loop(1, 4, several, 0)

    def ring_step(step):
        if step < 8:
            for j in (yl, other_y) if step > 2 else (other_y,):
                for k in range(PIECES):
                    for way in range(2):
                        ring_wait(way, step - 1, j, k)
                        ring_send(way, step, j, k)
        elif step == 8:
            for k in range(PIECES):
                for way in range(2):
                    ring_wait(way, 7, way, k)
                    ring_send(way, 8, way, k)
            for k in range(PIECES):
                for way in range(2):
                    ring_wait(way, 7, 1 - way, k)
        else:
            for k in range(PIECES):
                for way in range(2):
                    ring_wait(way, 8, way, k)

    def dout_done():
        arrived(dall.at[other_y], SEM["do"])
        flush(8)

    for step in range(2, 10):
        ring_step(step)
        if step == 2:
            tokens_second()
        if step == 6:
            tokens_mate()
        if step == 7:
            tokens_done()
            forward_first()
        if step == 8:
            for pair_step in range(4, 8):
                forward(pair_step)
            dout_done()
        if step == 9:
            forward(8)

    for device in later_peers:
        pl.semaphore_signal(barrier, inc=1, device_id=device, device_id_type=pl.DeviceIdType.MESH)

    def order(to, me):
        d = lax.rem(to - me + 6, 4)
        return lax.rem(2 * d, 5) - lax.div(d, 2) * (1 - lax.div(d, 3))

    scale = HEAD ** (-0.5)
    def attention():
        for i in range(2):
            rows = slice(SEQ * i, SEQ * i + SEQ)
            q_norm, q_inv = row_norm(acc[rows, 0:128])
            k_norm, k_inv = row_norm(acc[rows, 128:256])
            value = acc[rows, 256:384].astype(BF16)
            query, key = q_norm.astype(BF16), k_norm.astype(BF16)
            weights = jnp.exp(dot(query, key, 1, 1) * scale)
            probs = weights / jnp.sum(weights, axis=-1, keepdims=True)
            cot = dall[i]
            g_value = dot(probs.astype(BF16), cot, 0, 0)
            g_probs = dot(cot, value, 1, 1)
            g_scores = probs * (g_probs - jnp.sum(probs * g_probs, axis=-1, keepdims=True))
            g_scores = (g_scores * scale).astype(BF16)
            g_query = norm_backward(dot(g_scores, key), q_norm, q_inv)
            g_key = norm_backward(dot(g_scores, query, 0, 0), k_norm, k_inv)
            joined = jnp.concatenate([g_query, g_key, g_value], axis=1).astype(BF16)
            gls[c, :, SEQ * i : SEQ * i + SEQ] = dot(upad[...], joined, 1, 1)[0:RANK]
            if i == 0:
                b_part = dot(lowr[rows], joined, 0, 0)
            else:
                b_part = b_part + dot(lowr[rows], joined, 0, 0)
            for bh in range(2):
                for bx in range(4):
                    for bc in range(2):
                        r = 16 * (8 * bh + 2 * bx + bc)
                        by = 2 * bh + i
                        rel = lax.rem(c + bc, 2)
                        kx, ky = order(bx, x), order(by, y)
                        gj[0, rel, kx, ky] = joined[r : r + 16]
                        gj[1, rel, ky, kx] = joined[r : r + 16]
        return b_part[0:RANK]

    b_part = attention()
    send(gls.at[c], gls.at[c], SEM["g0"], mate)

    near = [(xs, ys), (ys, xs)]
    lo, hi = pl.ds(0, HP), pl.ds(HP, HP)

    def index(name, h, i, count, k):
        return SEM[name] + (h * PARTS + i) * count + k

    def to_mate(h, i, k):
        rows = (pl.ds(0, 1), pl.ds(1, 3))[k]
        send(sib_s.at[h, i, rows], sib_r.at[h, i, rows], index("sib", h, i, 2, k), mate)

    def from_mate(h, i, k):
        rows = (pl.ds(0, 1), pl.ds(1, 3))[k]
        arrived(sib_r.at[h, i, rows], index("sib", h, i, 2, k))

    def product(i):
        for h in range(2):
            right = wf[h, 4 * i : 4 * i + 4].reshape(PART, COLS)
            out = dot(gj[h].reshape(PLANE, COLS), right, 1, 1).reshape(2, 4, 4, 16, PART)
            sib_s[h, i] = out[1].astype(BF16)
            own[h, i] = out[0]
        for h in range(2):
            to_mate(h, i, 0)
            if i > 0:
                to_mate(h, i - 1, 1)
            if i == PARTS - 1:
                to_mate(h, i, 1)

    def stage_far(i):
        for h in range(2):
            from_mate(h, i, 0)
            far[h, i] = (own[h, i, 0] + sib_r[h, i, 0].astype(F32)).astype(BF16)
            send(far.at[h, i, :, :, lo], r1.at[h, i, 0], index("r1", h, i, 2, 0), near[h][0][0])
            send(far.at[h, i, :, :, hi], r1.at[h, i, 1], index("r1", h, i, 2, 1), near[h][0][2])

    def stage_near(i):
        for h in range(2):
            from_mate(h, i, 1)
            for k in range(2):
                arrived(r1.at[h, i, k], index("r1", h, i, 2, k))
                both = own[h, i, 1 + k] + sib_r[h, i, 1 + k].astype(F32)
                more = r1[h, i, k].astype(F32)
                if k == 0:
                    beside[h, i, k, :, :, 0:HP] = (both[:, :, 0:HP] + more).astype(BF16)
                    beside[h, i, k, :, :, HP:PART] = both[:, :, HP:PART].astype(BF16)
                else:
                    beside[h, i, k, :, :, 0:HP] = both[:, :, 0:HP].astype(BF16)
                    beside[h, i, k, :, :, HP:PART] = (both[:, :, HP:PART] + more).astype(BF16)
                send(beside.at[h, i, k], r2.at[h, i, k], index("r2", h, i, 2, k), near[h][0][2 * k])

    def columns(h, i):
        return slice(HALF * h + PART * i, HALF * h + PART * i + PART)

    def stage_own(i):
        for h in range(2):
            arrived(r2.at[h, i, 0], index("r2", h, i, 2, 0))
            arrived(r2.at[h, i, 1], index("r2", h, i, 2, 1))
            total = own[h, i, 3] + sib_r[h, i, 3].astype(F32) + r2[h, i, 0].astype(F32) + r2[h, i, 1].astype(F32)
            gn[:, columns(h, i)] += total[3]
            tot[h, i] = total[0:3].astype(BF16)
            for k, device in enumerate((near[h][1][1], near[h][1][0], near[h][1][2])):
                send(tot.at[h, i, k], r3.at[h, i, k], index("r3", h, i, 3, k), device)

    sums = [0.0, 0.0]

    def stage_last(i):
        for h in range(2):
            for k in range(3):
                arrived(r3.at[h, i, k], index("r3", h, i, 3, k))
            more = r3[h, i].astype(F32)
            cols = columns(h, i)
            grad = (gn[:, cols] + (more[0] + more[1] + more[2])) * gain[:, cols]
            gn[:, cols] = grad
            sums[0] += jnp.sum(grad, axis=-1, keepdims=True)
            sums[1] += jnp.sum(grad * xhat[:, cols], axis=-1, keepdims=True)

    factor = float(SEQ * 32) ** (-0.5)

    def spread(ref, slot, name, devices):
        for d in range(3):
            send(ref.at[slot], ref.at[slot], SEM[name] + d, devices[d])

    def gathered(ref, slot, name):
        for d in range(3):
            arrived(ref.at[lax.rem(slot + 3 - d, 4)], SEM[name] + d)

    def small(step):
        if step == 0:
            arrived(gls.at[other_c], SEM["g0"])
            glx[x] = gls[0] + gls[1]
            spread(glx, x, "g1", xs)
        if step == 1:
            gathered(glx, x, "g1")
            gly[y] = glx[0] + glx[1] + glx[2] + glx[3]
            spread(gly, y, "g2", ys)
        if step == 2:
            gathered(gly, y, "g2")
            low = gly[0] + gly[1] + gly[2] + gly[3]
            low = jnp.concatenate([low, jnp.zeros((8, PLANE), F32)], axis=0).astype(BF16)
            token = lax.broadcasted_iota(jnp.int32, (16, PLANE), 0) + (yl * SEQ + tt * 16)
            column = lax.broadcasted_iota(jnp.int32, (16, PLANE), 1)
            pick = jnp.where(token == column, 1.0, 0.0).astype(BF16)
            gn[...] = dot(dot(pick, low, 1, 1).astype(BF16), dpad[...])
            lanes = pl.ds(pl.multiple_of(384 * (4 * y + x), 128), 384)
            a_part = dot(low, norm[:, :, :, :, :, lanes].reshape(PLANE, 384))[0:RANK]
            z1[zl, 0:RANK] = a_part
            z1[zl, RANK : 2 * RANK] = b_part
            pl.semaphore_wait(barrier, len(later_peers))
            spread(z1, zl, "z1", zq)
        if step == 3:
            gathered(z1, zl, "z1")
            z2[zh] = z1[0] + z1[1] + z1[2] + z1[3]
            spread(z2, zh, "z2", zs)
        if step == 4:
            gathered(z2, zh, "z2")
            total = (z2[0] + z2[1] + z2[2] + z2[3]) * factor
            ga[y, x] = total[0:RANK]
            gb[yl] = total[RANK : 2 * RANK]
            send(gb.at[yl], gb.at[yl], SEM["by"], pair)
            for k, device in enumerate(across):
                send(ga.at[y, x], ga.at[y, x], SEM["ax"] + k, device)
        if step == 5:
            arrived(gb.at[other_y], SEM["by"])
            for h in range(2):
                for j in range(3):
                    o_b[:, 256 * j + 128 * h : 256 * j + 128 * h + 128] = gb[h, :, 128 * j : 128 * j + 128]
            for k, (a, b) in enumerate(plane):
                arrived(ga.at[lax.rem(y + 4 - a, 4), lax.rem(x + 4 - b, 4)], SEM["ax"] + k)
            for a in range(4):
                for b in range(4):
                    k = 384 * (4 * a + b)
                    o_a[:, k : k + 384] = ga[a, b]

    product(0)
    product(1)
    stage_far(0)
    small(0)
    product(2)
    stage_far(1)
    product(3)
    stage_far(2)
    stage_far(3)
    small(1)
    for i in range(PARTS):
        stage_near(i)
    flush(40)
    small(2)
    stage_own(0)
    small(3)
    stage_own(1)
    stage_own(2)
    small(4)
    stage_own(3)
    flush(54)
    stage_last(0)
    stage_last(1)
    small(5)
    flush(24)
    stage_last(2)
    stage_last(3)

    def finish():
        get_og.wait()
        first, second = sums[0] * (1.0 / WIDTH), sums[1] * (1.0 / WIDTH)
        out = (gn[...] - first - xhat[...] * second) * inv[:, 0:1]
        o_tok[...] = (og[...].astype(F32) + out).astype(BF16)

    finish()
    flush()


def copies(a, b, d, o_a, o_b, o_d):
    o_a[...] = a[...]
    o_b[...] = b[...]
    o_d[...] = d[...]


def per_device(tokens, gain, weight, down, up, out_gradient, att_gradient):
    vmem = pl.BlockSpec(memory_space=pltpu.VMEM)
    hbm = pl.BlockSpec(memory_space=pltpu.HBM)
    shapes = [
        ((16, WIDTH), BF16),
        ((1, WIDTH), F32),
        ((RANK, WIDTH), BF16),
        ((RANK, 2 * COLS), BF16),
        ((16, WIDTH), BF16),
        ((2, 2, 4, 2, 16, WIDTH), BF16),
        ((2, NZ, ROWS, COLS), BF16),
        ((PLANE, COLS), F32),
        ((2, SEQ, HEAD), BF16),
        ((16, WIDTH), F32),
        ((16, HEAD), F32),
        ((16, WIDTH), BF16),
        ((16, COLS), BF16),
        ((PLANE, 16), BF16),
        ((2, 2, 4, 4, 16, COLS), BF16),
        ((2, PARTS, 4, 4, 16, PART), BF16),
        ((2, PARTS, 4, 4, 16, PART), BF16),
        ((2, PARTS, 4, 4, 16, PART), F32),
        ((2, PARTS, 4, 16, PART), BF16),
        ((2, PARTS, 2, 4, 16, HP), BF16),
        ((2, PARTS, 2, 4, 16, PART), BF16),
        ((2, PARTS, 2, 4, 16, PART), BF16),
        ((2, PARTS, 3, 16, PART), BF16),
        ((2, PARTS, 3, 16, PART), BF16),
        ((16, WIDTH), F32),
        ((2, RANK, PLANE), F32),
        ((4, RANK, PLANE), F32),
        ((4, RANK, PLANE), F32),
        ((4, 2 * RANK, COLS), F32),
        ((4, 2 * RANK, COLS), F32),
        ((4, 4, RANK, 384), F32),
        ((2, RANK, COLS), F32),
    ]
    scratch = [pltpu.VMEM(shape, kind) for shape, kind in shapes]
    scratch += [pltpu.SemaphoreType.DMA((N_SEM,)), pltpu.SemaphoreType.DMA((N_SEM,)), pltpu.SemaphoreType.DMA((9,))]
    out_shape = (
        jax.ShapeDtypeStruct((16, WIDTH), BF16),
        jax.ShapeDtypeStruct((RANK, WIDTH), F32),
        jax.ShapeDtypeStruct((RANK, 2 * COLS), F32),
    )
    results = pl.pallas_call(
        kernel,
        out_shape=out_shape,
        in_specs=[hbm] * 7,
        out_specs=(vmem, vmem, vmem),
        scratch_shapes=scratch,
        compiler_params=pltpu.CompilerParams(
            collective_id=0, has_side_effects=True, vmem_limit_bytes=60 * 1024 * 1024
        ),
    )(tokens, gain.reshape(1, WIDTH), weight, down, up, out_gradient, att_gradient)
    return pl.pallas_call(
        copies,
        out_shape=out_shape,
        in_specs=[vmem] * 3,
        out_specs=(vmem, vmem, vmem),
    )(*results)


def solution(mesh):
    placed = (
        P(("dp", "tensor"), None),
        P(),
        P("dp", "tensor"),
        P(),
        P(None, "tensor"),
        P(("dp", "tensor"), None),
        P("dp", "tensor"),
    )
    return jax.shard_map(
        per_device,
        mesh=mesh,
        in_specs=placed,
        out_specs=(P(("dp", "tensor"), None), P(), P(None, "tensor")),
        check_vma=False,
    )
```

```python
import jax
import jax.numpy as jnp
from jax import lax
from jax.experimental import pallas as pl
from jax.experimental.pallas import tpu as pltpu
from jax.sharding import PartitionSpec as P

HEAD = 128
SEQ = 256
WIDTH = 6144
HALF = WIDTH // 2
RANK = 8
NZ = 16
ROWS = 192
COLS = 3 * HEAD
PIECES = 1
PARTS = 4
PART = HALF // PARTS
HP = PART // 2
PLANE = 512
EPSILON = 1e-06
F32 = jnp.float32
BF16 = jnp.bfloat16


def row_norm(values):
    mean = jnp.mean(values, axis=-1, keepdims=True)
    centred = values - mean
    inverse = lax.rsqrt(jnp.mean(centred * centred, axis=-1, keepdims=True) + EPSILON)
    return centred * inverse, inverse


def norm_backward(gradient, normal, inverse):
    return (
        gradient
        - jnp.mean(gradient, axis=-1, keepdims=True)
        - normal * jnp.mean(gradient * normal, axis=-1, keepdims=True)
    ) * inverse


def dot(a, b, ca=1, cb=0):
    return lax.dot_general(a, b, (((ca,), (cb,)), ((), ())), preferred_element_type=F32)


class Allocator:
    def __init__(self):
        self.size = 0

    def take(self, count):
        base = self.size
        self.size += count
        return base


def plan():
    al = Allocator()
    names = dict(
        wy=6, do=1, ring=64, t1=6, t2=6, t3=2,
        sib=4 * PARTS, r1=4 * PARTS, r2=4 * PARTS, r3=6 * PARTS,
        g0=1, g1=3, g2=3, z1=3, z2=3, ax=15, by=1,
    )
    bases = {name: al.take(count) for name, count in names.items()}
    return bases, al.size


SEM, N_SEM = plan()


def kernel(
    tok_in, gain_in, w_in, down_in, up_in, og_in, dout_in,
    o_tok, o_a, o_b,
    tok, gain, down, up, og,
    norm, wf, acc, dall, xhat, inv, dpad, upad, lowr,
    gj, sib_s, sib_r, own, far, r1, beside, r2, tot, r3, gn,
    gls, glx, gly, z1, z2, ga, gb,
    ssem, rsem, lsem,
):
    dp = lax.axis_index("dp")
    tt = lax.axis_index("tensor")
    yl, z = lax.div(dp, NZ), lax.rem(dp, NZ)
    yh = lax.div(tt, 8)
    x = lax.rem(lax.div(tt, 2), 4)
    c = lax.rem(tt, 2)
    y = 2 * yh + yl
    zh, zl = lax.div(z, 4), lax.rem(z, 4)
    other_c = 1 - c
    other_y = 1 - yl

    def at(y_, x_, z_, c_):
        return (
            lax.rem(y_, 2) * NZ + z_,
            lax.div(y_, 2) * 8 + x_ * 2 + c_,
        )

    xs = [at(y, lax.rem(x + d, 4), z, c) for d in (1, 2, 3)]
    ys = [at(lax.rem(y + d, 4), x, z, c) for d in (1, 2, 3)]
    zu = at(y, x, lax.rem(z + 1, NZ), c)
    zd = at(y, x, lax.rem(z + NZ - 1, NZ), c)
    zq = [at(y, x, zh * 4 + lax.rem(zl + d, 4), c) for d in (1, 2, 3)]
    zs = [at(y, x, lax.rem(zh + d, 4) * 4 + zl, c) for d in (1, 2, 3)]
    mate = at(y, x, z, other_c)
    pair = at(2 * yh + other_y, x, z, c)
    plane = [(a, b) for a in range(4) for b in range(4) if a + b > 0]
    across = [at(lax.rem(y + a, 4), lax.rem(x + b, 4), z, c) for a, b in plane]
    peers = [mate, *across, zu, zd]
    later_peers = [*zq, *zs]

    def copy(src, dst, k, device):
        return pltpu.make_async_remote_copy(
            src_ref=src, dst_ref=dst, send_sem=ssem.at[k], recv_sem=rsem.at[k],
            device_id=device, device_id_type=pl.DeviceIdType.MESH,
        )

    pending = []

    def send(src, dst, k, device):
        one = copy(src, dst, k, device)
        one.start()
        pending.append(one)

    def arrived(ref, k):
        copy(ref, ref, k, mate).wait_recv()

    def flush(keep=0):
        while len(pending) > keep:
            pending.pop(0).wait_send()

    barrier = pltpu.get_barrier_semaphore()
    for device in peers:
        pl.semaphore_signal(barrier, inc=1, device_id=device, device_id_type=pl.DeviceIdType.MESH)

    own_cols = pl.ds(pl.multiple_of(yl * HEAD, HEAD), HEAD)
    pair_cols = pl.ds(pl.multiple_of(other_y * HEAD, HEAD), HEAD)
    locals_ = []

    def fetch(src, dst):
        one = pltpu.make_async_copy(src, dst, lsem.at[len(locals_)])
        one.start()
        locals_.append(one)
        return one

    get_w = []
    for j in range(3):
        cols = pl.ds(pl.multiple_of(256 * j + yl * HEAD, HEAD), HEAD)
        get_w.append(fetch(w_in.at[:, cols], wf.at[yl, z, :, pl.ds(128 * j, 128)]))
    get_tok = [fetch(tok_in, tok), fetch(gain_in, gain)]
    get_small = [fetch(down_in, down), fetch(up_in, up), fetch(dout_in.at[:, own_cols], dall.at[yl])]
    get_og = fetch(og_in, og)

    for one in get_tok:
        one.wait()
    normal, inverse = row_norm(tok[...].astype(F32))
    xhat[...] = normal
    inv[...] = jnp.broadcast_to(inverse, inv.shape)
    norm[yl, yh, x, c] = (normal * gain[...]).astype(BF16)

    for one in get_small:
        one.wait()

    dpad[...] = jnp.concatenate([down[...].astype(F32), jnp.zeros((8, WIDTH), F32)], axis=0).astype(BF16)
    for j in range(3):
        cols = pl.ds(pl.multiple_of(256 * j + yl * HEAD, HEAD), HEAD)
        upad[:, 128 * j : 128 * j + 128] = jnp.concatenate(
            [up[:, cols].astype(F32), jnp.zeros((8, HEAD), F32)], axis=0
        ).astype(BF16)

    pl.semaphore_wait(barrier, len(peers))

    piece = ROWS // PIECES
    rows_of = [pl.ds(piece * k, piece) for k in range(PIECES)]
    for k in range(PIECES):
        for j in range(3):
            cols = pl.ds(pl.multiple_of(256 * j + other_y * HEAD, HEAD), HEAD)
            to = wf.at[yl, z, rows_of[k], pl.ds(128 * j, 128)]
            send(w_in.at[rows_of[k], cols], to, SEM["wy"] + 3 * k + j, pair)
    for one in get_w:
        one.wait()

    def ring_index(way, step, j, k):
        return SEM["ring"] + way * 32 + (step - 1) * 4 + 2 * j + k

    def ring_send(way, step, j, k):
        block = lax.rem(z + NZ - (step - 1), NZ) if way == 0 else lax.rem(z + step - 1, NZ)
        ref = wf.at[j, block, rows_of[k]]
        send(ref, ref, ring_index(way, step, j, k), zu if way == 0 else zd)

    def ring_wait(way, step, j, k):
        block = lax.rem(z + NZ - step, NZ) if way == 0 else lax.rem(z + step, NZ)
        arrived(wf.at[j, block, rows_of[k]], ring_index(way, step, j, k))

    for k in range(PIECES):
        for way in range(2):
            ring_send(way, 1, yl, k)
    a_cols, b_cols = pl.ds(0, HALF), pl.ds(HALF, HALF)
    a_ref = norm.at[yl, yh, x, c, :, a_cols]
    b_ref = norm.at[yl, yh, x, c, :, b_cols]
    for d in range(3):
        send(a_ref, a_ref, SEM["t1"] + d, xs[d])
        send(b_ref, b_ref, SEM["t1"] + 3 + d, ys[d])
    send(dout_in.at[:, pair_cols], dall.at[yl], SEM["do"], pair)
    for k in range(PIECES):
        for way in range(2):
            ring_wait(way, 1, yl, k)
            ring_send(way, 2, yl, k)
        for j in range(3):
            arrived(wf.at[other_y, z, rows_of[k], pl.ds(128 * j, 128)], SEM["wy"] + 3 * k + j)
        for way in range(2):
            ring_send(way, 1, other_y, k)

    def forward(step):
        up_way = lax.rem(step + z, 2)
        base = lax.rem(up_way * (z + step - 1) + (1 - up_way) * (z - step + NZ), NZ)
        block = lax.div(base, 2)
        left = []
        for j in range(2):
            lanes = pl.ds(pl.multiple_of(HALF * j + 2 * ROWS * block, 128), 2 * ROWS)
            left.append(norm[:, :, :, :, :, lanes].reshape(PLANE, 2 * ROWS))
        right = wf[:, pl.ds(2 * block, 2)].reshape(4 * ROWS, COLS)
        acc[...] += dot(jnp.concatenate(left, axis=1), right)

    def tokens_second():
        for d in range(3):
            xd, yd = lax.rem(x + 3 - d, 4), lax.rem(y + 3 - d, 4)
            arrived(norm.at[yl, yh, xd, c, :, a_cols], SEM["t1"] + d)
            arrived(norm.at[lax.rem(yd, 2), lax.div(yd, 2), x, c, :, b_cols], SEM["t1"] + 3 + d)
        ra = norm.at[yl, yh, :, c, :, a_cols]
        rb = norm.at[:, :, x, c, :, b_cols]
        for d in range(3):
            send(ra, ra, SEM["t2"] + d, ys[d])
            send(rb, rb, SEM["t2"] + 3 + d, xs[d])

    def tokens_mate():
        for d in range(3):
            yd = lax.rem(y + 3 - d, 4)
            arrived(norm.at[lax.rem(yd, 2), lax.div(yd, 2), :, c, :, a_cols], SEM["t2"] + d)
        ref = norm.at[:, :, :, c, :, a_cols]
        send(ref, ref, SEM["t3"], mate)
        for d in range(3):
            xd = lax.rem(x + 3 - d, 4)
            arrived(norm.at[:, :, xd, c, :, b_cols], SEM["t2"] + 3 + d)
        ref = norm.at[:, :, :, c, :, b_cols]
        send(ref, ref, SEM["t3"] + 1, mate)

    def tokens_done():
        arrived(norm.at[:, :, :, other_c, :, a_cols], SEM["t3"])
        arrived(norm.at[:, :, :, other_c, :, b_cols], SEM["t3"] + 1)

    def forward_first():
        low = dot(norm[...].reshape(PLANE, WIDTH), dpad[...], 1, 1).astype(BF16)
        lowr[...] = low
        acc[...] = dot(low, upad[...])

        def several(s, carry):
            forward(s)
            return carry

        lax.fori_loop(1, 4, several, 0)

    def ring_step(step):
        if step < 8:
            for j in (yl, other_y) if step > 2 else (other_y,):
                for k in range(PIECES):
                    for way in range(2):
                        ring_wait(way, step - 1, j, k)
                        ring_send(way, step, j, k)
        elif step == 8:
            for k in range(PIECES):
                for way in range(2):
                    ring_wait(way, 7, way, k)
                    ring_send(way, 8, way, k)
            for k in range(PIECES):
                for way in range(2):
                    ring_wait(way, 7, 1 - way, k)
        else:
            for k in range(PIECES):
                for way in range(2):
                    ring_wait(way, 8, way, k)

    def dout_done():
        arrived(dall.at[other_y], SEM["do"])
        flush(8)

    for step in range(2, 10):
        ring_step(step)
        if step == 2:
            tokens_second()
        if step == 6:
            tokens_mate()
        if step == 7:
            tokens_done()
            forward_first()
        if step == 8:
            for pair_step in range(4, 8):
                forward(pair_step)
            dout_done()
        if step == 9:
            forward(8)

    for device in later_peers:
        pl.semaphore_signal(barrier, inc=1, device_id=device, device_id_type=pl.DeviceIdType.MESH)

    def order(to, me):
        d = lax.rem(to - me + 6, 4)
        return lax.rem(2 * d, 5) - lax.div(d, 2) * (1 - lax.div(d, 3))

    scale = HEAD ** (-0.5)
    def attention():
        images = range(2)
        rows = [slice(SEQ * i, SEQ * i + SEQ) for i in images]
        q = [row_norm(acc[r, 0:128]) for r in rows]
        k = [row_norm(acc[r, 128:256]) for r in rows]
        value = [acc[r, 256:384].astype(BF16) for r in rows]
        query = [q[i][0].astype(BF16) for i in images]
        key = [k[i][0].astype(BF16) for i in images]
        weights = [jnp.exp(dot(query[i], key[i], 1, 1) * scale) for i in images]
        g_probs = [dot(dall[i], value[i], 1, 1) for i in images]
        probs = [weights[i] / jnp.sum(weights[i], axis=-1, keepdims=True) for i in images]
        g_value = [dot(probs[i].astype(BF16), dall[i], 0, 0) for i in images]
        inner = [jnp.sum(probs[i] * g_probs[i], axis=-1, keepdims=True) for i in images]
        g_scores = [(probs[i] * (g_probs[i] - inner[i]) * scale).astype(BF16) for i in images]
        g_query = [norm_backward(dot(g_scores[i], key[i]), *q[i]) for i in images]
        g_key = [norm_backward(dot(g_scores[i], query[i], 0, 0), *k[i]) for i in images]
        joined = [
            jnp.concatenate([g_query[i], g_key[i], g_value[i]], axis=1).astype(BF16) for i in images
        ]
        for i in images:
            gls[c, :, SEQ * i : SEQ * i + SEQ] = dot(upad[...], joined[i], 1, 1)[0:RANK]
        for i in images:
            for bh in range(2):
                for bx in range(4):
                    for bc in range(2):
                        r = 16 * (8 * bh + 2 * bx + bc)
                        by = 2 * bh + i
                        rel = lax.rem(c + bc, 2)
                        kx, ky = order(bx, x), order(by, y)
                        gj[0, rel, kx, ky] = joined[i][r : r + 16]
                        gj[1, rel, ky, kx] = joined[i][r : r + 16]
        b_part = dot(lowr[rows[0]], joined[0], 0, 0) + dot(lowr[rows[1]], joined[1], 0, 0)
        return b_part[0:RANK]

    b_part = attention()
    send(gls.at[c], gls.at[c], SEM["g0"], mate)

    near = [(xs, ys), (ys, xs)]
    lo, hi = pl.ds(0, HP), pl.ds(HP, HP)

    def index(name, h, i, count, k):
        return SEM[name] + (h * PARTS + i) * count + k

    def to_mate(h, i, k):
        rows = (pl.ds(0, 1), pl.ds(1, 3))[k]
        send(sib_s.at[h, i, rows], sib_r.at[h, i, rows], index("sib", h, i, 2, k), mate)

    def from_mate(h, i, k):
        rows = (pl.ds(0, 1), pl.ds(1, 3))[k]
        arrived(sib_r.at[h, i, rows], index("sib", h, i, 2, k))

    def product(i):
        for h in range(2):
            right = wf[h, 4 * i : 4 * i + 4].reshape(PART, COLS)
            out = dot(gj[h].reshape(PLANE, COLS), right, 1, 1).reshape(2, 4, 4, 16, PART)
            sib_s[h, i] = out[1].astype(BF16)
            own[h, i] = out[0]
        for h in range(2):
            to_mate(h, i, 0)
            if i > 0:
                to_mate(h, i - 1, 1)
            if i == PARTS - 1:
                to_mate(h, i, 1)

    def stage_far(i):
        for h in range(2):
            from_mate(h, i, 0)
            far[h, i] = (own[h, i, 0] + sib_r[h, i, 0].astype(F32)).astype(BF16)
            send(far.at[h, i, :, :, lo], r1.at[h, i, 0], index("r1", h, i, 2, 0), near[h][0][0])
            send(far.at[h, i, :, :, hi], r1.at[h, i, 1], index("r1", h, i, 2, 1), near[h][0][2])

    def stage_near(i):
        for h in range(2):
            from_mate(h, i, 1)
            for k in range(2):
                arrived(r1.at[h, i, k], index("r1", h, i, 2, k))
                both = own[h, i, 1 + k] + sib_r[h, i, 1 + k].astype(F32)
                more = r1[h, i, k].astype(F32)
                if k == 0:
                    beside[h, i, k, :, :, 0:HP] = (both[:, :, 0:HP] + more).astype(BF16)
                    beside[h, i, k, :, :, HP:PART] = both[:, :, HP:PART].astype(BF16)
                else:
                    beside[h, i, k, :, :, 0:HP] = both[:, :, 0:HP].astype(BF16)
                    beside[h, i, k, :, :, HP:PART] = (both[:, :, HP:PART] + more).astype(BF16)
                send(beside.at[h, i, k], r2.at[h, i, k], index("r2", h, i, 2, k), near[h][0][2 * k])

    def columns(h, i):
        return slice(HALF * h + PART * i, HALF * h + PART * i + PART)

    def stage_own(i):
        for h in range(2):
            arrived(r2.at[h, i, 0], index("r2", h, i, 2, 0))
            arrived(r2.at[h, i, 1], index("r2", h, i, 2, 1))
            total = own[h, i, 3] + sib_r[h, i, 3].astype(F32) + r2[h, i, 0].astype(F32) + r2[h, i, 1].astype(F32)
            gn[:, columns(h, i)] += total[3]
            tot[h, i] = total[0:3].astype(BF16)
            for k, device in enumerate((near[h][1][1], near[h][1][0], near[h][1][2])):
                send(tot.at[h, i, k], r3.at[h, i, k], index("r3", h, i, 3, k), device)

    sums = [0.0, 0.0]

    def stage_last(i):
        for h in range(2):
            for k in range(3):
                arrived(r3.at[h, i, k], index("r3", h, i, 3, k))
            more = r3[h, i].astype(F32)
            cols = columns(h, i)
            grad = (gn[:, cols] + (more[0] + more[1] + more[2])) * gain[:, cols]
            gn[:, cols] = grad
            sums[0] += jnp.sum(grad, axis=-1, keepdims=True)
            sums[1] += jnp.sum(grad * xhat[:, cols], axis=-1, keepdims=True)

    factor = float(SEQ * 32) ** (-0.5)

    def spread(ref, slot, name, devices):
        for d in range(3):
            send(ref.at[slot], ref.at[slot], SEM[name] + d, devices[d])

    def gathered(ref, slot, name):
        for d in range(3):
            arrived(ref.at[lax.rem(slot + 3 - d, 4)], SEM[name] + d)

    def small(step):
        if step == 0:
            arrived(gls.at[other_c], SEM["g0"])
            glx[x] = gls[0] + gls[1]
            spread(glx, x, "g1", xs)
        if step == 1:
            gathered(glx, x, "g1")
            gly[y] = glx[0] + glx[1] + glx[2] + glx[3]
            spread(gly, y, "g2", ys)
        if step == 2:
            gathered(gly, y, "g2")
            low = gly[0] + gly[1] + gly[2] + gly[3]
            low = jnp.concatenate([low, jnp.zeros((8, PLANE), F32)], axis=0).astype(BF16)
            token = lax.broadcasted_iota(jnp.int32, (16, PLANE), 0) + (yl * SEQ + tt * 16)
            column = lax.broadcasted_iota(jnp.int32, (16, PLANE), 1)
            pick = jnp.where(token == column, 1.0, 0.0).astype(BF16)
            gn[...] = dot(dot(pick, low, 1, 1).astype(BF16), dpad[...])
            lanes = pl.ds(pl.multiple_of(384 * (4 * y + x), 128), 384)
            a_part = dot(low, norm[:, :, :, :, :, lanes].reshape(PLANE, 384))[0:RANK]
            z1[zl, 0:RANK] = a_part
            z1[zl, RANK : 2 * RANK] = b_part
            pl.semaphore_wait(barrier, len(later_peers))
            spread(z1, zl, "z1", zq)
        if step == 3:
            gathered(z1, zl, "z1")
            z2[zh] = z1[0] + z1[1] + z1[2] + z1[3]
            spread(z2, zh, "z2", zs)
        if step == 4:
            gathered(z2, zh, "z2")
            total = (z2[0] + z2[1] + z2[2] + z2[3]) * factor
            ga[y, x] = total[0:RANK]
            gb[yl] = total[RANK : 2 * RANK]
            send(gb.at[yl], gb.at[yl], SEM["by"], pair)
            for k, device in enumerate(across):
                send(ga.at[y, x], ga.at[y, x], SEM["ax"] + k, device)
        if step == 5:
            arrived(gb.at[other_y], SEM["by"])
            for h in range(2):
                for j in range(3):
                    o_b[:, 256 * j + 128 * h : 256 * j + 128 * h + 128] = gb[h, :, 128 * j : 128 * j + 128]
            for k, (a, b) in enumerate(plane):
                arrived(ga.at[lax.rem(y + 4 - a, 4), lax.rem(x + 4 - b, 4)], SEM["ax"] + k)
            for a in range(4):
                for b in range(4):
                    k = 384 * (4 * a + b)
                    o_a[:, k : k + 384] = ga[a, b]

    product(0)
    product(1)
    stage_far(0)
    small(0)
    product(2)
    stage_far(1)
    product(3)
    stage_far(2)
    stage_far(3)
    small(1)
    for i in range(PARTS):
        stage_near(i)
    flush(40)
    small(2)
    stage_own(0)
    small(3)
    stage_own(1)
    stage_own(2)
    small(4)
    stage_own(3)
    flush(54)
    stage_last(0)
    stage_last(1)
    small(5)
    flush(24)
    stage_last(2)
    stage_last(3)

    def finish():
        get_og.wait()
        first, second = sums[0] * (1.0 / WIDTH), sums[1] * (1.0 / WIDTH)
        out = (gn[...] - first - xhat[...] * second) * inv[:, 0:1]
        o_tok[...] = (og[...].astype(F32) + out).astype(BF16)

    finish()
    flush()


def copies(a, b, d, o_a, o_b, o_d):
    o_a[...] = a[...]
    o_b[...] = b[...]
    o_d[...] = d[...]


def per_device(tokens, gain, weight, down, up, out_gradient, att_gradient):
    vmem = pl.BlockSpec(memory_space=pltpu.VMEM)
    hbm = pl.BlockSpec(memory_space=pltpu.HBM)
    shapes = [
        ((16, WIDTH), BF16),
        ((1, WIDTH), F32),
        ((RANK, WIDTH), BF16),
        ((RANK, 2 * COLS), BF16),
        ((16, WIDTH), BF16),
        ((2, 2, 4, 2, 16, WIDTH), BF16),
        ((2, NZ, ROWS, COLS), BF16),
        ((PLANE, COLS), F32),
        ((2, SEQ, HEAD), BF16),
        ((16, WIDTH), F32),
        ((16, HEAD), F32),
        ((16, WIDTH), BF16),
        ((16, COLS), BF16),
        ((PLANE, 16), BF16),
        ((2, 2, 4, 4, 16, COLS), BF16),
        ((2, PARTS, 4, 4, 16, PART), BF16),
        ((2, PARTS, 4, 4, 16, PART), BF16),
        ((2, PARTS, 4, 4, 16, PART), F32),
        ((2, PARTS, 4, 16, PART), BF16),
        ((2, PARTS, 2, 4, 16, HP), BF16),
        ((2, PARTS, 2, 4, 16, PART), BF16),
        ((2, PARTS, 2, 4, 16, PART), BF16),
        ((2, PARTS, 3, 16, PART), BF16),
        ((2, PARTS, 3, 16, PART), BF16),
        ((16, WIDTH), F32),
        ((2, RANK, PLANE), F32),
        ((4, RANK, PLANE), F32),
        ((4, RANK, PLANE), F32),
        ((4, 2 * RANK, COLS), F32),
        ((4, 2 * RANK, COLS), F32),
        ((4, 4, RANK, 384), F32),
        ((2, RANK, COLS), F32),
    ]
    scratch = [pltpu.VMEM(shape, kind) for shape, kind in shapes]
    scratch += [pltpu.SemaphoreType.DMA((N_SEM,)), pltpu.SemaphoreType.DMA((N_SEM,)), pltpu.SemaphoreType.DMA((9,))]
    out_shape = (
        jax.ShapeDtypeStruct((16, WIDTH), BF16),
        jax.ShapeDtypeStruct((RANK, WIDTH), F32),
        jax.ShapeDtypeStruct((RANK, 2 * COLS), F32),
    )
    results = pl.pallas_call(
        kernel,
        out_shape=out_shape,
        in_specs=[hbm] * 7,
        out_specs=(vmem, vmem, vmem),
        scratch_shapes=scratch,
        compiler_params=pltpu.CompilerParams(
            collective_id=0, has_side_effects=True, vmem_limit_bytes=60 * 1024 * 1024
        ),
    )(tokens, gain.reshape(1, WIDTH), weight, down, up, out_gradient, att_gradient)
    return pl.pallas_call(
        copies,
        out_shape=out_shape,
        in_specs=[vmem] * 3,
        out_specs=(vmem, vmem, vmem),
    )(*results)


def solution(mesh):
    placed = (
        P(("dp", "tensor"), None),
        P(),
        P("dp", "tensor"),
        P(),
        P(None, "tensor"),
        P(("dp", "tensor"), None),
        P("dp", "tensor"),
    )
    return jax.shard_map(
        per_device,
        mesh=mesh,
        in_specs=placed,
        out_specs=(P(("dp", "tensor"), None), P(), P(None, "tensor")),
        check_vma=False,
    )
```
